32 devices in a mesh: leaf: 32 (over z, y, x, core).
Axes of the slice: x: 2, y: 2, z: 4, core: 2. Of those that a mesh axis runs over, the one named last changes fastest.
Arguments:
- right_hand: float32 [512, 32, 256], P('leaf')
- leaf_live: int32 [512], P('leaf'), may hold values from 0 to 1, as said below
- near_index: int32 [512, 6], P('leaf'), may hold values from 0 to 511, as said below
- near_tile: bfloat16 [512, 6, 256, 256], P('leaf'), may hold values from -1 to 5
- far_index: int32 [512, 8], P('leaf'), may hold values from 0 to 511, as said below
- far_couple: bfloat16 [512, 8, 64, 64], P('leaf'), may hold values from -0.25 to 0.25
- leaf_basis: bfloat16 [512, 64, 256], P('leaf'), may hold values from -0.375 to 0.375
- leaf_transfer: bfloat16 [512, 64, 64], P('leaf'), may hold values from -0.1875 to 0.1875
- tree_up: bfloat16 [62, 64, 64], replicated, may hold values from -0.5 to 0.5
- tree_couple: bfloat16 [62, 64, 64], replicated, may hold values from -0.75 to 0.75
Outputs:
- basis_next: float32 [512, 32, 256], P('leaf')
- hessenberg: float32 [6, 32], replicated
The draws below stay inside these ranges and needn't reach their ends.
Inputs may be any that keep to these rules, and one draw needn't show every extreme that they name: `leaf_live`: each device's 16 slots hold between 5 and 16 live leaves, both counts reached on some device; which slots are live is arbitrary. `near_index`: entry 0 of each row is the row's own slot; every entry lies within 2 slots of its row's slot, and some entry lies exactly 2 away; entries may name dead slots. `far_index`: every entry lies within 16 slots of its row's slot, and some entry lies exactly 16 away; entries may name dead slots.
All inputs are finite; a program needn't handle non-finite values.
Results may differ from the reference program's by a relative error of at most 0.009.
Values may be sent and summed in bfloat16 or wider, within the bound.
A program may use at most 128 MiB of HBM per device.

```python
import math
import jax
import jax.numpy as jnp
from jax import lax

P_SIZE = 256
K = 64
R = 32
NEAR = 6
FAR = 8
REACH = 2
LEAF_DEV = 16
LEAVES = 512
NODES = 62
LEVELS = 5
N_LEAF = 32


def draw_right_hand(key, part):
    key_base = jax.random.fold_in(jax.random.fold_in(key, 11), 0)
    key_column = jax.random.fold_in(jax.random.fold_in(key, 11), 1)
    key_point = jax.random.fold_in(jax.random.fold_in(key, 11), 2)
    key_tilt = jax.random.fold_in(jax.random.fold_in(key, 11), 4)
    slot_pos = jnp.arange(LEAVES, dtype=jnp.float32) / (LEAVES - 1)
    column_scale = jnp.exp(jax.random.uniform(key_column, (R,), jnp.float32) * math.log(10.0))
    point_scale = jnp.exp(jax.random.uniform(key_point, (LEAVES, 1, P_SIZE), jnp.float32) * math.log(3.0))
    values = jax.random.normal(key_base, (LEAVES, R, P_SIZE), jnp.float32)
    power = jax.random.uniform(key_tilt, (R,), jnp.float32, 0.5, 3.0)
    rising = jnp.exp(jnp.log(1.0 + 2.0 * slot_pos)[:, None] * power[None, :])
    mean_square = (jnp.exp((2.0 * power + 1.0) * math.log(3.0)) - 1.0) / (2.0 * (2.0 * power + 1.0))
    rising = rising / jnp.sqrt(mean_square)[None, :]
    overall = 0.15 / math.sqrt(LEAVES * P_SIZE)
    return overall * values * point_scale * rising[:, :, None] * column_scale[None, :, None]


def draw_near_tile(key, part):
    key_noise, key_diag = jax.random.split(jax.random.fold_in(key, 13))
    spread = 1.0 / math.sqrt(NEAR * P_SIZE)
    slot_pos = jnp.arange(LEAVES, dtype=jnp.float32) / (LEAVES - 1)
    noise = jax.random.truncated_normal(key_noise, -4.0, 4.0, (LEAVES, NEAR, P_SIZE, P_SIZE), jnp.float32) * spread
    weights = jnp.exp(math.log(0.15) + jax.random.uniform(key_diag, (LEAVES, P_SIZE), jnp.float32) * math.log(10.0))
    trend = 0.3 + 1.7 * slot_pos
    smoothing = weights * trend[:, None]
    own_tile = (jnp.arange(NEAR) == 0)[None, :, None, None]
    on_diagonal = (jnp.arange(P_SIZE)[:, None] == jnp.arange(P_SIZE)[None, :])[None, None, :, :]
    tiles = noise + jnp.where(own_tile & on_diagonal, smoothing[:, None, None, :], 0.0)
    return tiles.astype(jnp.bfloat16)


def draw_leaf_live(key, part):
    key_count, key_full, key_empty, key_perm = jax.random.split(jax.random.fold_in(key, 3), 4)
    lowest = max(1, LEAF_DEV // 3)
    counts = jax.random.randint(key_count, (N_LEAF,), lowest, LEAF_DEV + 1)
    full_dev = jax.random.randint(key_full, (), 0, N_LEAF)
    empty_dev = (full_dev + 1 + jax.random.randint(key_empty, (), 0, N_LEAF - 1)) % N_LEAF
    counts = counts.at[full_dev].set(LEAF_DEV).at[empty_dev].set(lowest)
    ranks = jax.vmap(lambda subkey: jax.random.permutation(subkey, LEAF_DEV))(jax.random.split(key_perm, N_LEAF))
    return (ranks < counts[:, None]).astype(jnp.int32).reshape(-1)


def draw_near_index(key, part):
    offsets = jax.random.randint(jax.random.fold_in(key, 5), (LEAVES, NEAR), -REACH, REACH + 1)
    offsets = offsets.at[:, 0].set(0).at[LEAF_DEV, 1].set(-REACH)
    rows = jnp.arange(LEAVES, dtype=jnp.int32)[:, None]
    return jnp.clip(rows + offsets, 0, LEAVES - 1).astype(jnp.int32)


def draw_far_index(key, part):
    key_size, key_sign = jax.random.split(jax.random.fold_in(key, 7))
    magnitude = jax.random.randint(key_size, (LEAVES, FAR), REACH + 1, LEAF_DEV + 1)
    signs = jax.random.randint(key_sign, (LEAVES, FAR), 0, 2) * 2 - 1
    offsets = magnitude * signs
    offsets = offsets.at[LEAF_DEV, 0].set(-LEAF_DEV).at[LEAVES - 1 - LEAF_DEV, 0].set(LEAF_DEV)
    rows = jnp.arange(LEAVES, dtype=jnp.int32)[:, None]
    return jnp.clip(rows + offsets, 0, LEAVES - 1).astype(jnp.int32)


def block_scale(rng, shape, cuts, least, largest):
    factor_of = 1.0
    for axis_at, shards_of in cuts:
        draws = jax.random.uniform(jax.random.fold_in(jax.random.fold_in(rng, 6), axis_at), (shards_of,), jnp.float32, least / len(cuts), largest / len(cuts))
        factor_of = factor_of * jnp.repeat(jnp.exp(draws), shape[axis_at] // shards_of).reshape((-1,) + (1,) * (len(shape) - 1 - axis_at))
    return factor_of


def centred(stream_key, shape, deviation, limit, cuts=(), kind=jnp.bfloat16):
    entries = deviation * jax.random.normal(stream_key, shape, jnp.float32)
    if cuts:
        entries = entries * block_scale(stream_key, shape, cuts, -0.22, 0.18)
    return jnp.clip(entries, -limit, limit).astype(kind)


def setup_inputs(seed: int = 0) -> dict:
    streams_of = jax.random.split(jax.random.key(seed), 11)
    right_hand = draw_right_hand(jax.random.fold_in(streams_of[10], 71), 0)
    leaf_live = draw_leaf_live(jax.random.fold_in(streams_of[10], 71), 0)
    near_index = draw_near_index(jax.random.fold_in(streams_of[10], 71), 0)
    near_tile = draw_near_tile(jax.random.fold_in(streams_of[10], 71), 0)
    far_index = draw_far_index(jax.random.fold_in(streams_of[10], 71), 0)
    far_couple = centred(streams_of[5], (LEAVES, FAR, K, K), (FAR * K) ** -0.5, 0.25, ((0, 32),))
    leaf_basis = centred(streams_of[6], (LEAVES, K, P_SIZE), P_SIZE ** -0.5, 0.375, ((0, 32),))
    leaf_transfer = centred(streams_of[7], (LEAVES, K, K), (LEAF_DEV * K) ** -0.5, 0.1875, ((0, 32),))
    tree_up = centred(streams_of[8], (NODES, K, K), (2 * K) ** -0.5, 0.5)
    tree_couple = centred(streams_of[9], (NODES, K, K), K ** -0.5, 0.75)
    return dict(right_hand=right_hand, leaf_live=leaf_live, near_index=near_index, near_tile=near_tile, far_index=far_index, far_couple=far_couple, leaf_basis=leaf_basis, leaf_transfer=leaf_transfer, tree_up=tree_up, tree_couple=tree_couple)


epsilon = 1e-06

def level_start(level):
    return 2 * N_LEAF - 2 * (N_LEAF >> level)

def apply_operator(vector, leaf_live, near_index, near_tile, far_index, far_couple, leaf_basis, leaf_transfer, tree_up, tree_couple):
    live_mask = leaf_live.astype(jnp.float32)[:, None, None]
    inputs = (vector * live_mask).astype(jnp.bfloat16)

    def near_block(pieces):
        block_index, block_tiles = pieces
        columns = inputs[block_index].astype(jnp.float32)
        return jnp.einsum('inrp,inpq->irq', columns, block_tiles.astype(jnp.float32))
    near = lax.map(near_block, (near_index.reshape(N_LEAF, LEAF_DEV, NEAR), near_tile.reshape(N_LEAF, LEAF_DEV, NEAR, P_SIZE, P_SIZE)))
    near = near.reshape(LEAVES, R, P_SIZE)
    moments = jnp.einsum('irp,ikp->irk', inputs.astype(jnp.float32), leaf_basis.astype(jnp.float32)).astype(jnp.bfloat16)
    far_term = jnp.einsum('ifrk,ifkj->irj', moments[far_index].astype(jnp.float32), far_couple.astype(jnp.float32))
    transfer_dev = leaf_transfer.reshape(N_LEAF, LEAF_DEV, K, K).astype(jnp.float32)
    coarse = jnp.einsum('dirk,dikj->drj', moments.reshape(N_LEAF, LEAF_DEV, R, K).astype(jnp.float32), transfer_dev).astype(jnp.bfloat16)
    locals_list = []
    for level in range(LEVELS):
        width_now = N_LEAF >> level
        first = level_start(level)
        swapped = coarse.reshape(width_now // 2, 2, R, K)[:, ::-1].reshape(width_now, R, K)
        locals_list.append(jnp.einsum('nrk,nkj->nrj', swapped.astype(jnp.float32), tree_couple[first:first + width_now].astype(jnp.float32)))
        lifted = jnp.einsum('nrk,nkj->nrj', coarse.astype(jnp.float32), tree_up[first:first + width_now].astype(jnp.float32))
        coarse = (lifted[0::2] + lifted[1::2]).astype(jnp.bfloat16)
    downward = jnp.zeros((1, R, K), jnp.bfloat16)
    for level in reversed(range(LEVELS)):
        width_now = N_LEAF >> level
        first = level_start(level)
        parent = jnp.repeat(downward, 2, axis=0)
        carried = jnp.einsum('nrj,nkj->nrk', parent.astype(jnp.float32), tree_up[first:first + width_now].astype(jnp.float32))
        downward = (locals_list[level] + carried).astype(jnp.bfloat16)
    leaf_down = jnp.einsum('drj,dikj->dirk', downward.astype(jnp.float32), transfer_dev).reshape(LEAVES, R, K)
    local_total = (far_term + leaf_down).astype(jnp.bfloat16)
    spread = jnp.einsum('irk,ikp->irp', local_total.astype(jnp.float32), leaf_basis.astype(jnp.float32))
    return live_mask * (near + spread)

def column_sums(first_field, second_field):
    return lax.optimization_barrier(jnp.sum(first_field * second_field, axis=(0, 2)))

def reference(right_hand, leaf_live, near_index, near_tile, far_index, far_couple, leaf_basis, leaf_transfer, tree_up, tree_couple):

    def operator(vector):
        return apply_operator(vector, leaf_live, near_index, near_tile, far_index, far_couple, leaf_basis, leaf_transfer, tree_up, tree_couple)
    live_mask = leaf_live.astype(jnp.float32)[:, None, None]
    start_vec = right_hand * live_mask
    norm_start = jnp.sqrt(column_sums(start_vec, start_vec) + epsilon)
    basis_one = start_vec / norm_start[None, :, None]
    image_one = operator(basis_one)
    first_inner = column_sums(basis_one, image_one)
    residue_one = image_one - first_inner[None, :, None] * basis_one
    first_length = jnp.sqrt(column_sums(residue_one, residue_one) + epsilon)
    basis_two = residue_one / first_length[None, :, None]
    image_two = operator(basis_two)
    cross_inner = column_sums(basis_one, image_two)
    self_inner = column_sums(basis_two, image_two)
    residue_two = image_two - cross_inner[None, :, None] * basis_one - self_inner[None, :, None] * basis_two
    second_length = jnp.sqrt(column_sums(residue_two, residue_two) + epsilon)
    basis_next = residue_two / second_length[None, :, None]
    hessenberg = jnp.stack([norm_start, first_inner, first_length, cross_inner, self_inner, second_length])
    return (basis_next, hessenberg)
```

```python
import functools
import jax
import jax.numpy as jnp
from jax import lax
from jax.experimental import pallas as pl
from jax.experimental.pallas import tpu as pltpu
from jax.sharding import PartitionSpec as P

epsilon = 1e-06
GROUP = 8
F32 = jnp.float32
BF16 = jnp.bfloat16


def dot(a, b):
    return jnp.dot(a, b, preferred_element_type=F32)


def dot_nt(a, b):
    return lax.dot_general(a, b, (((1,), (1,)), ((), ())), preferred_element_type=F32)


def to_columns(rows):
    return jnp.transpose(jnp.concatenate([rows] * 16, axis=0))


def kernel(
    n,
    live_ref,
    near_idx,
    far_idx,
    rhs_hbm,
    near_hbm,
    far_hbm,
    basis_hbm,
    transfer_hbm,
    up_hbm,
    couple_hbm,
    out_ref,
    hess_ref,
    rhs,
    near_t,
    far_t,
    basis,
    transfer,
    up,
    couple,
    own_0,
    own_1,
    full_0,
    full_1,
    mom_0,
    mom_1,
    local,
    w1,
    w2,
    weight_a,
    weight_b,
    twice,
    gat_a,
    gat_b,
    red_a,
    red_b,
    load_sem,
    near_sem,
    halo_send,
    halo_recv,
    a_send,
    a_recv,
    b_send,
    b_recv,
    ra_send,
    ra_recv,
    rb_send,
    rb_recv,
):
    slots, cols, points = rhs.shape
    own, full, mom = (own_0, own_1), (full_0, full_1), (mom_0, mom_1)
    rank = basis.shape[1]
    reach = (full_0.shape[0] - slots) // 2
    near_count = near_idx.shape[1]
    far_count = far_idx.shape[1]
    groups = n // GROUP
    levels = n.bit_length() - 1
    low = GROUP.bit_length() - 1
    me = lax.axis_index("leaf")
    j = me % GROUP
    base = me - j
    q = me // GROUP

    def load(hbm, vmem, k):
        return pltpu.make_async_copy(hbm, vmem, load_sem.at[k])

    loads = [
        load(rhs_hbm, rhs, 0),
        load(basis_hbm, basis, 1),
        load(transfer_hbm, transfer, 2),
        load(up_hbm, up, 3),
        load(couple_hbm, couple, 4),
        load(far_hbm, far_t, 5),
    ]
    for c in loads[:5]:
        c.start()

    def near_load(i):
        return pltpu.make_async_copy(near_hbm.at[i], near_t.at[i], near_sem.at[i])

    def start_near(i, carry):
        near_load(i).start()
        return carry

    lax.fori_loop(0, slots, start_near, 0)
    loads[5].start()

    for a in range(2):
        full[a][0:reach] = jnp.zeros((reach, cols, points), BF16)
        full[a][reach + slots : slots + 2 * reach] = jnp.zeros((reach, cols, points), BF16)
        mom[a][0:slots] = jnp.zeros((slots, cols, 2 * rank), BF16)
        mom[a][2 * slots : 3 * slots] = jnp.zeros((slots, cols, 2 * rank), BF16)

    barrier = pltpu.get_barrier_semaphore()

    def greet(dev):
        pl.semaphore_signal(barrier, inc=1, device_id=(dev,), device_id_type=pl.DeviceIdType.MESH)

    for k in range(1, GROUP):
        greet(base + (j + k) % GROUP)
    for k in range(1, groups):
        greet(((q + k) % groups) * GROUP + j)
    greet((me + 1) % n)
    greet((me + n - 1) % n)

    def remote(src, dst, send_sem, recv_sem, dev):
        return pltpu.make_async_remote_copy(
            src_ref=src,
            dst_ref=dst,
            send_sem=send_sem,
            recv_sem=recv_sem,
            device_id=(dev,),
            device_id_type=pl.DeviceIdType.MESH,
        )

    def copies_a(buf, s, r):
        return [
            remote(buf.at[j], buf.at[j], s.at[k - 1], r.at[k - 1], base + (j + k) % GROUP)
            for k in range(1, GROUP)
        ]

    def copies_b(buf, s, r):
        return [
            remote(buf.at[q], buf.at[q], s.at[k - 1], r.at[k - 1], ((q + k) % groups) * GROUP + j)
            for k in range(1, groups)
        ]

    def arrive_a(buf, s, r):
        for k in range(1, GROUP):
            src = (j + GROUP - k) % GROUP
            remote(buf.at[src], buf.at[src], s.at[k - 1], r.at[k - 1], base + src).wait_recv()

    def arrive_b(buf, s, r):
        for k in range(1, groups):
            src = (q + groups - k) % groups
            remote(
                buf.at[src], buf.at[src], s.at[k - 1], r.at[k - 1], src * GROUP + j
            ).wait_recv()

    def halo(a, kind):
        if kind == 0:
            up_src, up_dst = own[a].at[slots - reach : slots], full[a].at[0:reach]
            dn_src = own[a].at[0:reach]
            dn_dst = full[a].at[reach + slots : slots + 2 * reach]
        else:
            up_src, up_dst = mom[a].at[slots : 2 * slots], mom[a].at[0:slots]
            dn_src, dn_dst = mom[a].at[slots : 2 * slots], mom[a].at[2 * slots : 3 * slots]
        to_up = remote(up_src, up_dst, halo_send.at[a, kind, 0], halo_recv.at[a, kind, 0], (me + 1) % n)
        to_dn = remote(
            dn_src, dn_dst, halo_send.at[a, kind, 1], halo_recv.at[a, kind, 1], (me + n - 1) % n
        )
        return to_up, to_dn

    def halo_start(a, kind):
        to_up, to_dn = halo(a, kind)
        pl.when(me < n - 1)(to_up.start)
        pl.when(me > 0)(to_dn.start)

    def halo_arrive(a, kind):
        to_up, to_dn = halo(a, kind)
        pl.when(me > 0)(to_up.wait_recv)
        pl.when(me < n - 1)(to_dn.wait_recv)

    def halo_finish(a, kind):
        to_up, to_dn = halo(a, kind)
        pl.when(me < n - 1)(to_up.wait_send)
        pl.when(me > 0)(to_dn.wait_send)

    lane = lax.broadcasted_iota(jnp.int32, (cols, 2 * rank), 1)
    left_half = lane < rank

    def pair(x, y):
        return jnp.where(left_half, x, y)

    def halved(dup, parity):
        keep = (lane // rank) == parity
        return jnp.where(keep, dup, 0.0).astype(BF16)

    def moment_loop(a):
        def step(t, carry):
            i0 = t * 4
            got = []
            for u in range(4):
                b = basis[i0 + u]
                got.append(dot_nt(own[a][i0 + u], jnp.concatenate([b, b], axis=0)).astype(BF16))
            for u in range(4):
                mom[a][slots + i0 + u] = got[u]
            return carry

        lax.fori_loop(0, slots // 4, step, 0)

    def box_start(a):
        flat = jnp.concatenate(
            [pair(mom[a][slots + 2 * p], mom[a][slots + 2 * p + 1]) for p in range(slots // 2)],
            axis=1,
        )
        gat_a[a, j] = halved(dot(flat, twice[...]), j % 2)
        for c in copies_a(gat_a.at[a], a_send.at[a], a_recv.at[a]):
            c.start()

    def near_rows(a, rows, wait_tiles, src, shift):
        got = []
        first = me * slots - shift
        last = src[a].shape[0] - 1
        for i in rows:
            if wait_tiles:
                near_load(i).wait()
            v = jnp.concatenate(
                [src[a][jnp.clip(near_idx[i, k] - first, 0, last)] for k in range(near_count)], axis=1
            )
            got.append(dot(v, near_t[i].reshape(near_count * points, points)))
        for i, g in zip(rows, got):
            w2[i] = g

    def near_inner(a, lo, hi):
        def step(t, carry):
            i0 = lo + t * 4
            near_rows(a, [i0 + u for u in range(4)], a == 0, own, 0)
            return carry

        lax.fori_loop(0, (hi - lo) // 4, step, 0)

    def group_round(a):
        arrive_a(gat_a.at[a], a_send.at[a], a_recv.at[a])
        cat = jnp.concatenate(
            [gat_a[a, 2 * p] + gat_a[a, 2 * p + 1] for p in range(GROUP // 2)], axis=1
        )
        got = dot(cat, weight_a[...])
        gat_b[a, q] = halved(got[:, 2 * rank : 4 * rank], q % 2)
        for c in copies_b(gat_b.at[a], b_send.at[a], b_recv.at[a]):
            c.start()
        return got[:, : 2 * rank]

    def cross_round(a, part):
        arrive_b(gat_b.at[a], b_send.at[a], b_recv.at[a])
        cat = jnp.concatenate(
            [gat_b[a, 2 * p] + gat_b[a, 2 * p + 1] for p in range(groups // 2)], axis=1
        )
        total = part + dot(cat, weight_b[...])[:, : 2 * rank]
        return total[:, :rank].astype(BF16)

    def far_loop(a, down):
        first = me * slots - slots

        def source(i, f):
            return mom[a][jnp.clip(far_idx[i, f] - first, 0, 3 * slots - 1)]

        def step(t, carry):
            got = []
            for u in range(4):
                i = t * 4 + u
                v = jnp.concatenate(
                    [
                        pair(source(i, 2 * p), source(i, 2 * p + 1))
                        for p in range(far_count // 2)
                    ],
                    axis=1,
                )
                tr = transfer[pl.ds(pl.multiple_of(i * rank, rank), rank), :]
                got.append((dot(v, far_t[i]) + dot_nt(down, tr)).astype(BF16))
            for u in range(4):
                local[t * 4 + u] = got[u]
            return carry

        lax.fori_loop(0, slots // 4, step, 0)

    def spread(i):
        mask = live_ref[i].astype(F32)
        return (w2[i] + dot(local[i], basis[i])) * mask

    def fold(x):
        return x[:, : points // 2] + x[:, points // 2 :]

    def pack(parts):
        wide = lax.broadcasted_iota(jnp.int32, (cols, 128), 1)
        total = jnp.zeros((cols, 128), F32)
        for k, p in enumerate(parts):
            total = total + jnp.where(wide == k, jnp.sum(p, axis=1, keepdims=True), 0.0)
        padded = jnp.concatenate([total, jnp.zeros((128 - cols, 128), F32)], axis=0)
        return jnp.transpose(padded)[:8]

    def reduce_first(t, rows):
        red_a[t, j] = rows
        for c in copies_a(red_a.at[t], ra_send.at[t], ra_recv.at[t]):
            c.start()

    def reduce_second(t):
        arrive_a(red_a.at[t], ra_send.at[t], ra_recv.at[t])
        total = red_a[t, 0]
        for k in range(1, GROUP):
            total = total + red_a[t, k]
        red_b[t, q] = total
        for c in copies_b(red_b.at[t], rb_send.at[t], rb_recv.at[t]):
            c.start()

    def reduce_third(t):
        arrive_b(red_b.at[t], rb_send.at[t], rb_recv.at[t])
        total = red_b[t, 0]
        for k in range(1, groups):
            total = total + red_b[t, k]
        return total

    loads[0].wait()

    def start_step(i, acc):
        s = rhs[i] * live_ref[i].astype(F32)
        rhs[i] = s
        v = s.astype(BF16)
        own[0][i] = v
        full[0][reach + i] = v
        return acc + fold(s * s)

    norm_part = lax.fori_loop(0, slots, start_step, jnp.zeros((cols, points // 2), F32))
    pl.semaphore_wait(barrier, GROUP - 1 + groups - 1 + 2)
    halo_start(0, 0)
    loads[1].wait()
    moment_loop(0)
    halo_start(0, 1)

    rowi = lax.broadcasted_iota(jnp.int32, (rank, 2 * rank), 0)
    coli = lax.broadcasted_iota(jnp.int32, (rank, 2 * rank), 1)
    eye_twice = jnp.where(rowi == coli % rank, 1.0, 0.0).astype(BF16)
    loads[2].wait()
    twice[...] = dot(transfer[...], eye_twice).astype(BF16)
    box_start(0)
    reduce_first(0, pack([norm_part]))

    loads[3].wait()
    loads[4].wait()

    def node_row(level, node):
        return pl.multiple_of((2 * n - 2 * (n >> level) + node) * rank, rank)

    def node_up(level, node, count):
        return up[pl.ds(node_row(level, node), count * rank), :]

    path = None
    couples = []
    for level in range(levels):
        c = couple[pl.ds(node_row(level, me >> level), rank), :]
        if path is None:
            r4 = lax.broadcasted_iota(jnp.int32, (4 * rank, rank), 0)
            c4 = lax.broadcasted_iota(jnp.int32, (4 * rank, rank), 1)
            path_pad = jnp.where(r4 == c4, 1.0, 0.0).astype(BF16)
        else:
            path_pad = jnp.concatenate([path, jnp.zeros((3 * rank, rank), BF16)], axis=0)
        couples.append(dot_nt(c, path_pad))
        if level < levels - 1:
            u = node_up(level, me >> level, 1)
            path = u if path is None else dot(path, u).astype(BF16)

    def own_sibling(level, node):
        sibling = (me >> level) ^ 1
        f0 = jnp.where(sibling == node, 1.0, 0.0).astype(F32)
        f1 = jnp.where(sibling == node + 1, 1.0, 0.0).astype(F32)
        return jnp.concatenate([couples[level] * f0, couples[level] * f1], axis=0)

    wide_r = lax.broadcasted_iota(jnp.int32, (rank, 4 * rank), 0)
    wide_c = lax.broadcasted_iota(jnp.int32, (rank, 4 * rank), 1)
    root = jnp.where((wide_c >= 2 * rank) & (wide_r == wide_c % rank), 1.0, 0.0).astype(BF16)
    nodes = [root]
    for level in reversed(range(low)):
        below = []
        for m, x in enumerate(nodes):
            node = (base >> level) + 2 * m
            both = (dot(node_up(level, node, 2), x) + own_sibling(level, node)).astype(BF16)
            below.extend([both[:rank], both[rank:]])
        nodes = below
    for k, x in enumerate(nodes):
        weight_a[k * rank : (k + 1) * rank, :] = x
    nodes = [None]
    for level in reversed(range(low, levels)):
        below = []
        for m, x in enumerate(nodes):
            both = own_sibling(level, 2 * m)
            if x is not None:
                both = both + dot(node_up(level, 2 * m, 2), x)
            both = both.astype(BF16)
            below.extend([both[:rank], both[rank:]])
        nodes = below
    for k, x in enumerate(nodes):
        weight_b[k * rank : (k + 1) * rank, :] = x

    def operator_middle(a):
        near_inner(a, reach, reach + 4)
        part = group_round(a)
        if a == 0:
            reduce_second(0)
        near_inner(a, reach + 4, slots - reach)
        halo_arrive(a, 0)
        near_rows(a, [0, 1, slots - 2, slots - 1], a == 0, full, reach)
        down = cross_round(a, part)
        if a == 0:
            loads[5].wait()
        halo_arrive(a, 1)
        far_loop(a, down)

    operator_middle(0)
    norm_row = jnp.sqrt(reduce_third(0) + epsilon)
    inv_norm = to_columns(1.0 / norm_row)[:cols, 0:1]
    own_square = red_b[0, 0]
    for k in range(1, groups):
        own_square = own_square + red_b[0, k]

    def image_step(t, carry):
        got = [spread(t * 4 + u) * inv_norm for u in range(4)]
        for u in range(4):
            i = t * 4 + u
            v = got[u].astype(BF16)
            w1[i] = got[u]
            own[1][i] = v
            full[1][reach + i] = v
        return carry

    lax.fori_loop(0, slots // 4, image_step, 0)
    halo_start(1, 0)
    moment_loop(1)
    halo_start(1, 1)
    box_start(1)
    operator_middle(1)

    def gram_step(t, accs):
        got = [spread(t * 4 + u) for u in range(4)]
        for u in range(4):
            i = t * 4 + u
            z = got[u]
            w2[i] = z
            b = rhs[i] * inv_norm
            w = w1[i]
            accs = (
                accs[0] + fold(b * w),
                accs[1] + fold(w * w),
                accs[2] + fold(b * z),
                accs[3] + fold(w * z),
                accs[4] + fold(z * z),
            )
        return accs

    zero = jnp.zeros((cols, points // 2), F32)
    accs = lax.fori_loop(0, slots // 4, gram_step, (zero,) * 5)
    reduce_first(1, pack(accs))
    reduce_second(1)
    sums = reduce_third(1)

    norm = norm_row[0:1]
    unit = own_square[0:1] / (norm * norm)
    h, e, f, g, k2 = (sums[k : k + 1] for k in range(5))
    first_square = jnp.maximum(e - 2.0 * h * h + h * h * unit, 0.0)
    length = jnp.sqrt(first_square + epsilon)
    inv_l = 1.0 / length
    cross = (f - h * h) * inv_l
    inner = (g - h * e - h * f + h * h * h) * inv_l * inv_l
    image_square = (k2 - 2.0 * h * g + h * h * e) * inv_l * inv_l
    second_square = (
        image_square
        - 2.0 * cross * cross
        - 2.0 * inner * inner
        + cross * cross * unit
        + inner * inner * first_square * inv_l * inv_l
        + 2.0 * cross * inner * (h - h * unit) * inv_l
    )
    second = jnp.sqrt(jnp.maximum(second_square, 0.0) + epsilon)
    inv_s = 1.0 / second
    alpha = inv_l * inv_s
    beta = -(h + inner) * alpha
    gamma = (inner * h * inv_l - cross) * inv_s / norm
    blank = jnp.zeros((1, 128), F32)
    hess = jnp.concatenate([norm, h, length, cross, inner, second, blank, blank], axis=0)
    hess_ref[...] = hess[:6, :cols]
    coef = to_columns(jnp.concatenate([alpha, beta, gamma] + [blank] * 5, axis=0))
    ca, cb, cg = (coef[:cols, k : k + 1] for k in range(3))

    def out_step(i, carry):
        out_ref[i] = ca * w2[i] + cb * w1[i] + cg * rhs[i]
        return carry

    lax.fori_loop(0, slots, out_step, 0)

    for a in range(2):
        for c in copies_a(gat_a.at[a], a_send.at[a], a_recv.at[a]):
            c.wait_send()
        for c in copies_b(gat_b.at[a], b_send.at[a], b_recv.at[a]):
            c.wait_send()
        for c in copies_a(red_a.at[a], ra_send.at[a], ra_recv.at[a]):
            c.wait_send()
        for c in copies_b(red_b.at[a], rb_send.at[a], rb_recv.at[a]):
            c.wait_send()
        halo_finish(a, 0)
        halo_finish(a, 1)


def on_device(
    right_hand,
    leaf_live,
    near_index,
    near_tile,
    far_index,
    far_couple,
    leaf_basis,
    leaf_transfer,
    tree_up,
    tree_couple,
):
    n = lax.axis_size("leaf")
    slots, cols, points = right_hand.shape
    rank = leaf_basis.shape[1]
    far_count = far_index.shape[1]
    nodes = tree_up.shape[0]
    reach = 2
    groups = n // GROUP
    far_flat = far_couple.reshape(slots, far_count * rank, rank)
    transfer_flat = leaf_transfer.reshape(slots * rank, rank)
    up_flat = tree_up.reshape(nodes * rank, rank)
    couple_flat = tree_couple.reshape(nodes * rank, rank)
    smem = pl.BlockSpec(memory_space=pltpu.SMEM)
    anywhere = pl.BlockSpec(memory_space=pl.ANY)
    vmem = pl.BlockSpec(memory_space=pltpu.VMEM)
    dma = pltpu.SemaphoreType.DMA
    return pl.pallas_call(
        functools.partial(kernel, n),
        out_shape=(
            jax.ShapeDtypeStruct((slots, cols, points), F32),
            jax.ShapeDtypeStruct((6, cols), F32),
        ),
        in_specs=[smem] * 3 + [anywhere] * 7,
        out_specs=(vmem, vmem),
        scratch_shapes=[
            pltpu.VMEM((slots, cols, points), F32),
            pltpu.VMEM(near_tile.shape, BF16),
            pltpu.VMEM(far_flat.shape, BF16),
            pltpu.VMEM(leaf_basis.shape, BF16),
            pltpu.VMEM(transfer_flat.shape, BF16),
            pltpu.VMEM(up_flat.shape, BF16),
            pltpu.VMEM(couple_flat.shape, BF16),
            pltpu.VMEM((slots, cols, points), BF16),
            pltpu.VMEM((slots, cols, points), BF16),
            pltpu.VMEM((slots + 2 * reach, cols, points), BF16),
            pltpu.VMEM((slots + 2 * reach, cols, points), BF16),
            pltpu.VMEM((3 * slots, cols, 2 * rank), BF16),
            pltpu.VMEM((3 * slots, cols, 2 * rank), BF16),
            pltpu.VMEM((slots, cols, rank), BF16),
            pltpu.VMEM((slots, cols, points), F32),
            pltpu.VMEM((slots, cols, points), F32),
            pltpu.VMEM((GROUP * rank, 4 * rank), BF16),
            pltpu.VMEM((groups * rank, 4 * rank), BF16),
            pltpu.VMEM((slots * rank, 2 * rank), BF16),
            pltpu.VMEM((2, GROUP, cols, 2 * rank), BF16),
            pltpu.VMEM((2, groups, cols, 2 * rank), BF16),
            pltpu.VMEM((2, GROUP, 8, 128), F32),
            pltpu.VMEM((2, groups, 8, 128), F32),
            dma((6,)),
            dma((slots,)),
            dma((2, 2, 2)),
            dma((2, 2, 2)),
            dma((2, GROUP - 1)),
            dma((2, GROUP - 1)),
            dma((2, groups - 1)),
            dma((2, groups - 1)),
            dma((2, GROUP - 1)),
            dma((2, GROUP - 1)),
            dma((2, groups - 1)),
            dma((2, groups - 1)),
        ],
        compiler_params=pltpu.CompilerParams(
            collective_id=0, has_side_effects=True, vmem_limit_bytes=40 * 1024 * 1024
        ),
    )(
        leaf_live,
        near_index,
        far_index,
        right_hand,
        near_tile,
        far_flat,
        leaf_basis,
        transfer_flat,
        up_flat,
        couple_flat,
    )


def solution(mesh):
    placed = (
        P("leaf", None, None),
        P("leaf"),
        P("leaf", None),
        P("leaf", None, None, None),
        P("leaf", None),
        P("leaf", None, None, None),
        P("leaf", None, None),
        P("leaf", None, None),
        P(),
        P(),
    )
    return jax.shard_map(
        on_device,
        mesh=mesh,
        in_specs=placed,
        out_specs=(P("leaf", None, None), P()),
        check_vma=False,
    )
```

```python
import functools
import jax
import jax.numpy as jnp
from jax import lax
from jax.experimental import pallas as pl
from jax.experimental.pallas import tpu as pltpu
from jax.sharding import PartitionSpec as P

epsilon = 1e-06
GROUP = 8
F32 = jnp.float32
BF16 = jnp.bfloat16


def dot(a, b):
    return jnp.dot(a, b, preferred_element_type=F32)


def dot_nt(a, b):
    return lax.dot_general(a, b, (((1,), (1,)), ((), ())), preferred_element_type=F32)


def to_columns(rows):
    return jnp.transpose(jnp.concatenate([rows] * 16, axis=0))


def kernel(
    n,
    live_ref,
    near_idx,
    far_idx,
    rhs_hbm,
    near_hbm,
    far_hbm,
    basis_hbm,
    transfer_hbm,
    up_hbm,
    couple_hbm,
    out_ref,
    hess_ref,
    rhs,
    near_t,
    far_t,
    basis,
    transfer,
    up,
    couple,
    own_0,
    own_1,
    full_0,
    full_1,
    mom_0,
    mom_1,
    local,
    w1,
    w2,
    weight_a,
    weight_b,
    twice,
    gat_a,
    gat_b,
    red_a,
    red_b,
    load_sem,
    near_sem,
    halo_send,
    halo_recv,
    a_send,
    a_recv,
    b_send,
    b_recv,
    ra_send,
    ra_recv,
    rb_send,
    rb_recv,
):
    slots, cols, points = rhs.shape
    own, full, mom = (own_0, own_1), (full_0, full_1), (mom_0, mom_1)
    rank = basis.shape[1]
    reach = (full_0.shape[0] - slots) // 2
    near_count = near_idx.shape[0]
    far_count = far_idx.shape[0]
    groups = n // GROUP
    levels = n.bit_length() - 1
    low = GROUP.bit_length() - 1
    me = lax.axis_index("leaf")
    j = me % GROUP
    base = me - j
    q = me // GROUP

    def load(hbm, vmem, k):
        return pltpu.make_async_copy(hbm, vmem, load_sem.at[k])

    loads = [
        load(rhs_hbm, rhs, 0),
        load(basis_hbm, basis, 1),
        load(transfer_hbm, transfer, 2),
        load(up_hbm, up, 3),
        load(couple_hbm, couple, 4),
        load(far_hbm, far_t, 5),
    ]
    for c in loads[:5]:
        c.start()

    def near_load(i):
        return pltpu.make_async_copy(near_hbm.at[i], near_t.at[i], near_sem.at[i])

    def start_near(i, carry):
        near_load(i).start()
        return carry

    lax.fori_loop(0, slots, start_near, 0)
    loads[5].start()

    for a in range(2):
        full[a][0:reach] = jnp.zeros((reach, cols, points), BF16)
        full[a][reach + slots : slots + 2 * reach] = jnp.zeros((reach, cols, points), BF16)
        mom[a][0:slots] = jnp.zeros((slots, cols, 2 * rank), BF16)
        mom[a][2 * slots : 3 * slots] = jnp.zeros((slots, cols, 2 * rank), BF16)

    barrier = pltpu.get_barrier_semaphore()

    def greet(dev):
        pl.semaphore_signal(barrier, inc=1, device_id=(dev,), device_id_type=pl.DeviceIdType.MESH)

    for k in range(1, GROUP):
        greet(base + (j + k) % GROUP)
    for k in range(1, groups):
        greet(((q + k) % groups) * GROUP + j)
    greet((me + 1) % n)
    greet((me + n - 1) % n)

    def remote(src, dst, send_sem, recv_sem, dev):
        return pltpu.make_async_remote_copy(
            src_ref=src,
            dst_ref=dst,
            send_sem=send_sem,
            recv_sem=recv_sem,
            device_id=(dev,),
            device_id_type=pl.DeviceIdType.MESH,
        )

    def copies_a(buf, s, r):
        return [
            remote(buf.at[j], buf.at[j], s.at[k - 1], r.at[k - 1], base + (j + k) % GROUP)
            for k in range(1, GROUP)
        ]

    def copies_b(buf, s, r):
        return [
            remote(buf.at[q], buf.at[q], s.at[k - 1], r.at[k - 1], ((q + k) % groups) * GROUP + j)
            for k in range(1, groups)
        ]

    def arrive_a(buf, s, r):
        for k in range(1, GROUP):
            src = (j + GROUP - k) % GROUP
            remote(buf.at[src], buf.at[src], s.at[k - 1], r.at[k - 1], base + src).wait_recv()

    def arrive_b(buf, s, r):
        for k in range(1, groups):
            src = (q + groups - k) % groups
            remote(
                buf.at[src], buf.at[src], s.at[k - 1], r.at[k - 1], src * GROUP + j
            ).wait_recv()

    def halo(a, kind):
        if kind == 0:
            up_src, up_dst = own[a].at[slots - reach : slots], full[a].at[0:reach]
            dn_src = own[a].at[0:reach]
            dn_dst = full[a].at[reach + slots : slots + 2 * reach]
        else:
            up_src, up_dst = mom[a].at[slots : 2 * slots], mom[a].at[0:slots]
            dn_src, dn_dst = mom[a].at[slots : 2 * slots], mom[a].at[2 * slots : 3 * slots]
        to_up = remote(up_src, up_dst, halo_send.at[a, kind, 0], halo_recv.at[a, kind, 0], (me + 1) % n)
        to_dn = remote(
            dn_src, dn_dst, halo_send.at[a, kind, 1], halo_recv.at[a, kind, 1], (me + n - 1) % n
        )
        return to_up, to_dn

    def halo_start(a, kind):
        to_up, to_dn = halo(a, kind)
        pl.when(me < n - 1)(to_up.start)
        pl.when(me > 0)(to_dn.start)

    def halo_arrive(a, kind):
        to_up, to_dn = halo(a, kind)
        pl.when(me > 0)(to_up.wait_recv)
        pl.when(me < n - 1)(to_dn.wait_recv)

    def halo_finish(a, kind):
        to_up, to_dn = halo(a, kind)
        pl.when(me < n - 1)(to_up.wait_send)
        pl.when(me > 0)(to_dn.wait_send)

    lane = lax.broadcasted_iota(jnp.int32, (cols, 2 * rank), 1)
    left_half = lane < rank

    def pair(x, y):
        return jnp.where(left_half, x, y)

    def halved(dup, parity):
        keep = (lane // rank) == parity
        return jnp.where(keep, dup, 0.0).astype(BF16)

    def moment_loop(a):
        def step(t, carry):
            i0 = t * 8
            got = []
            for u in range(8):
                b = basis[i0 + u]
                got.append(dot_nt(own[a][i0 + u], jnp.concatenate([b, b], axis=0)).astype(BF16))
            for u in range(8):
                mom[a][slots + i0 + u] = got[u]
            return carry

        lax.fori_loop(0, slots // 8, step, 0)

    def box_start(a):
        flat = jnp.concatenate(
            [pair(mom[a][slots + 2 * p], mom[a][slots + 2 * p + 1]) for p in range(slots // 2)],
            axis=1,
        )
        gat_a[a, j] = halved(dot(flat, twice[...]), j % 2)
        for c in copies_a(gat_a.at[a], a_send.at[a], a_recv.at[a]):
            c.start()

    def near_rows(a, rows, wait_tiles, src, shift):
        got = []
        first = me * slots - shift
        last = src[a].shape[0] - 1
        for i in rows:
            if wait_tiles:
                near_load(i).wait()
            v = jnp.concatenate(
                [src[a][jnp.clip(near_idx[k, i] - first, 0, last)] for k in range(near_count)], axis=1
            )
            got.append(dot(v, near_t[i].reshape(near_count * points, points)))
        for i, g in zip(rows, got):
            w2[i] = g

    def near_inner(a, lo, hi):
        def step(t, carry):
            i0 = lo + t * 4
            near_rows(a, [i0 + u for u in range(4)], a == 0, own, 0)
            return carry

        lax.fori_loop(0, (hi - lo) // 4, step, 0)

    def group_round(a):
        arrive_a(gat_a.at[a], a_send.at[a], a_recv.at[a])
        cat = jnp.concatenate(
            [gat_a[a, 2 * p] + gat_a[a, 2 * p + 1] for p in range(GROUP // 2)], axis=1
        )
        got = dot(cat, weight_a[...])
        gat_b[a, q] = halved(got[:, 2 * rank : 4 * rank], q % 2)
        for c in copies_b(gat_b.at[a], b_send.at[a], b_recv.at[a]):
            c.start()
        return got[:, : 2 * rank]

    def cross_round(a, part):
        arrive_b(gat_b.at[a], b_send.at[a], b_recv.at[a])
        cat = jnp.concatenate(
            [gat_b[a, 2 * p] + gat_b[a, 2 * p + 1] for p in range(groups // 2)], axis=1
        )
        total = part + dot(cat, weight_b[...])[:, : 2 * rank]
        return total[:, :rank].astype(BF16)

    def far_loop(a, down):
        first = me * slots - slots

        def source(i, f):
            return mom[a][jnp.clip(far_idx[f, i] - first, 0, 3 * slots - 1)]

        def step(t, carry):
            got = []
            for u in range(8):
                i = t * 8 + u
                v = jnp.concatenate(
                    [
                        pair(source(i, 2 * p), source(i, 2 * p + 1))
                        for p in range(far_count // 2)
                    ],
                    axis=1,
                )
                tr = transfer[pl.ds(pl.multiple_of(i * rank, rank), rank), :]
                got.append((dot(v, far_t[i]) + dot_nt(down, tr)).astype(BF16))
            for u in range(8):
                local[t * 8 + u] = got[u]
            return carry

        lax.fori_loop(0, slots // 8, step, 0)

    def spread(i):
        mask = live_ref[i].astype(F32)
        return (w2[i] + dot(local[i], basis[i])) * mask

    def fold(x):
        return x[:, : points // 2] + x[:, points // 2 :]

    def pack(parts):
        wide = lax.broadcasted_iota(jnp.int32, (cols, 128), 1)
        total = jnp.zeros((cols, 128), F32)
        for k, p in enumerate(parts):
            total = total + jnp.where(wide == k, jnp.sum(p, axis=1, keepdims=True), 0.0)
        padded = jnp.concatenate([total, jnp.zeros((128 - cols, 128), F32)], axis=0)
        return jnp.transpose(padded)[:8]

    def reduce_first(t, rows):
        red_a[t, j] = rows
        for c in copies_a(red_a.at[t], ra_send.at[t], ra_recv.at[t]):
            c.start()

    def reduce_second(t):
        arrive_a(red_a.at[t], ra_send.at[t], ra_recv.at[t])
        total = red_a[t, 0]
        for k in range(1, GROUP):
            total = total + red_a[t, k]
        red_b[t, q] = total
        for c in copies_b(red_b.at[t], rb_send.at[t], rb_recv.at[t]):
            c.start()

    def reduce_third(t):
        arrive_b(red_b.at[t], rb_send.at[t], rb_recv.at[t])
        total = red_b[t, 0]
        for k in range(1, groups):
            total = total + red_b[t, k]
        return total

    loads[0].wait()

    def start_step(i, acc):
        s = rhs[i] * live_ref[i].astype(F32)
        rhs[i] = s
        v = s.astype(BF16)
        own[0][i] = v
        full[0][reach + i] = v
        return acc + fold(s * s)

    norm_part = lax.fori_loop(0, slots, start_step, jnp.zeros((cols, points // 2), F32))
    pl.semaphore_wait(barrier, GROUP - 1 + groups - 1 + 2)
    halo_start(0, 0)
    loads[1].wait()
    moment_loop(0)
    halo_start(0, 1)

    rowi = lax.broadcasted_iota(jnp.int32, (rank, 2 * rank), 0)
    coli = lax.broadcasted_iota(jnp.int32, (rank, 2 * rank), 1)
    eye_twice = jnp.where(rowi == coli % rank, 1.0, 0.0).astype(BF16)
    loads[2].wait()
    twice[...] = dot(transfer[...], eye_twice).astype(BF16)
    box_start(0)
    reduce_first(0, pack([norm_part]))

    loads[3].wait()
    loads[4].wait()

    def node_row(level, node):
        return pl.multiple_of((2 * n - 2 * (n >> level) + node) * rank, rank)

    def node_up(level, node, count):
        return up[pl.ds(node_row(level, node), count * rank), :]

    path = None
    couples = []
    for level in range(levels):
        c = couple[pl.ds(node_row(level, me >> level), rank), :]
        if path is None:
            r4 = lax.broadcasted_iota(jnp.int32, (4 * rank, rank), 0)
            c4 = lax.broadcasted_iota(jnp.int32, (4 * rank, rank), 1)
            path_pad = jnp.where(r4 == c4, 1.0, 0.0).astype(BF16)
        else:
            path_pad = jnp.concatenate([path, jnp.zeros((3 * rank, rank), BF16)], axis=0)
        couples.append(dot_nt(c, path_pad))
        if level < levels - 1:
            u = node_up(level, me >> level, 1)
            path = u if path is None else dot(path, u).astype(BF16)

    def own_sibling(level, node):
        sibling = (me >> level) ^ 1
        f0 = jnp.where(sibling == node, 1.0, 0.0).astype(F32)
        f1 = jnp.where(sibling == node + 1, 1.0, 0.0).astype(F32)
        return jnp.concatenate([couples[level] * f0, couples[level] * f1], axis=0)

    wide_r = lax.broadcasted_iota(jnp.int32, (rank, 4 * rank), 0)
    wide_c = lax.broadcasted_iota(jnp.int32, (rank, 4 * rank), 1)
    root = jnp.where((wide_c >= 2 * rank) & (wide_r == wide_c % rank), 1.0, 0.0).astype(BF16)
    nodes = [root]
    for level in reversed(range(low)):
        below = []
        for m, x in enumerate(nodes):
            node = (base >> level) + 2 * m
            both = (dot(node_up(level, node, 2), x) + own_sibling(level, node)).astype(BF16)
            below.extend([both[:rank], both[rank:]])
        nodes = below
    for k, x in enumerate(nodes):
        weight_a[k * rank : (k + 1) * rank, :] = x
    nodes = [None]
    for level in reversed(range(low, levels)):
        below = []
        for m, x in enumerate(nodes):
            both = own_sibling(level, 2 * m)
            if x is not None:
                both = both + dot(node_up(level, 2 * m, 2), x)
            both = both.astype(BF16)
            below.extend([both[:rank], both[rank:]])
        nodes = below
    for k, x in enumerate(nodes):
        weight_b[k * rank : (k + 1) * rank, :] = x

    def operator_middle(a):
        near_inner(a, reach, reach + 4)
        part = group_round(a)
        if a == 0:
            reduce_second(0)
        near_inner(a, reach + 4, slots - reach)
        halo_arrive(a, 0)
        near_rows(a, [0, 1, slots - 2, slots - 1], a == 0, full, reach)
        down = cross_round(a, part)
        if a == 0:
            loads[5].wait()
        halo_arrive(a, 1)
        far_loop(a, down)

    operator_middle(0)
    norm_row = jnp.sqrt(reduce_third(0) + epsilon)
    inv_norm = to_columns(1.0 / norm_row)[:cols, 0:1]
    own_square = red_b[0, 0]
    for k in range(1, groups):
        own_square = own_square + red_b[0, k]

    def image_step(t, carry):
        got = [spread(t * 4 + u) * inv_norm for u in range(4)]
        for u in range(4):
            i = t * 4 + u
            v = got[u].astype(BF16)
            w1[i] = got[u]
            own[1][i] = v
            full[1][reach + i] = v
        return carry

    lax.fori_loop(0, slots // 4, image_step, 0)
    halo_start(1, 0)
    moment_loop(1)
    halo_start(1, 1)
    box_start(1)
    operator_middle(1)

    def gram_step(t, accs):
        got = [spread(t * 4 + u) for u in range(4)]
        for u in range(4):
            i = t * 4 + u
            z = got[u]
            w2[i] = z
            b = rhs[i] * inv_norm
            w = w1[i]
            accs = (
                accs[0] + fold(b * w),
                accs[1] + fold(w * w),
                accs[2] + fold(b * z),
                accs[3] + fold(w * z),
                accs[4] + fold(z * z),
            )
        return accs

    zero = jnp.zeros((cols, points // 2), F32)
    accs = lax.fori_loop(0, slots // 4, gram_step, (zero,) * 5)
    reduce_first(1, pack(accs))
    reduce_second(1)
    sums = reduce_third(1)

    norm = norm_row[0:1]
    unit = own_square[0:1] / (norm * norm)
    h, e, f, g, k2 = (sums[k : k + 1] for k in range(5))
    first_square = jnp.maximum(e - 2.0 * h * h + h * h * unit, 0.0)
    length = jnp.sqrt(first_square + epsilon)
    inv_l = 1.0 / length
    cross = (f - h * h) * inv_l
    inner = (g - h * e - h * f + h * h * h) * inv_l * inv_l
    image_square = (k2 - 2.0 * h * g + h * h * e) * inv_l * inv_l
    second_square = (
        image_square
        - 2.0 * cross * cross
        - 2.0 * inner * inner
        + cross * cross * unit
        + inner * inner * first_square * inv_l * inv_l
        + 2.0 * cross * inner * (h - h * unit) * inv_l
    )
    second = jnp.sqrt(jnp.maximum(second_square, 0.0) + epsilon)
    inv_s = 1.0 / second
    alpha = inv_l * inv_s
    beta = -(h + inner) * alpha
    gamma = (inner * h * inv_l - cross) * inv_s / norm
    blank = jnp.zeros((1, 128), F32)
    hess = jnp.concatenate([norm, h, length, cross, inner, second, blank, blank], axis=0)
    hess_ref[...] = hess[:6, :cols]
    coef = to_columns(jnp.concatenate([alpha, beta, gamma] + [blank] * 5, axis=0))
    ca, cb, cg = (coef[:cols, k : k + 1] for k in range(3))

    def out_step(i, carry):
        out_ref[i] = ca * w2[i] + cb * w1[i] + cg * rhs[i]
        return carry

    lax.fori_loop(0, slots, out_step, 0)

    for a in range(2):
        for c in copies_a(gat_a.at[a], a_send.at[a], a_recv.at[a]):
            c.wait_send()
        for c in copies_b(gat_b.at[a], b_send.at[a], b_recv.at[a]):
            c.wait_send()
        for c in copies_a(red_a.at[a], ra_send.at[a], ra_recv.at[a]):
            c.wait_send()
        for c in copies_b(red_b.at[a], rb_send.at[a], rb_recv.at[a]):
            c.wait_send()
        halo_finish(a, 0)
        halo_finish(a, 1)


def on_device(
    right_hand,
    leaf_live,
    near_index,
    near_tile,
    far_index,
    far_couple,
    leaf_basis,
    leaf_transfer,
    tree_up,
    tree_couple,
):
    n = lax.axis_size("leaf")
    slots, cols, points = right_hand.shape
    rank = leaf_basis.shape[1]
    far_count = far_index.shape[1]
    nodes = tree_up.shape[0]
    reach = 2
    groups = n // GROUP
    far_flat = far_couple.reshape(slots, far_count * rank, rank)
    transfer_flat = leaf_transfer.reshape(slots * rank, rank)
    up_flat = tree_up.reshape(nodes * rank, rank)
    couple_flat = tree_couple.reshape(nodes * rank, rank)
    smem = pl.BlockSpec(memory_space=pltpu.SMEM)
    anywhere = pl.BlockSpec(memory_space=pltpu.HBM)
    vmem = pl.BlockSpec(memory_space=pltpu.VMEM)
    dma = pltpu.SemaphoreType.DMA
    return pl.pallas_call(
        functools.partial(kernel, n),
        out_shape=(
            jax.ShapeDtypeStruct((slots, cols, points), F32),
            jax.ShapeDtypeStruct((6, cols), F32),
        ),
        in_specs=[smem] * 3 + [anywhere] * 7,
        out_specs=(vmem, vmem),
        scratch_shapes=[
            pltpu.VMEM((slots, cols, points), F32),
            pltpu.VMEM(near_tile.shape, BF16),
            pltpu.VMEM(far_flat.shape, BF16),
            pltpu.VMEM(leaf_basis.shape, BF16),
            pltpu.VMEM(transfer_flat.shape, BF16),
            pltpu.VMEM(up_flat.shape, BF16),
            pltpu.VMEM(couple_flat.shape, BF16),
            pltpu.VMEM((slots, cols, points), BF16),
            pltpu.VMEM((slots, cols, points), BF16),
            pltpu.VMEM((slots + 2 * reach, cols, points), BF16),
            pltpu.VMEM((slots + 2 * reach, cols, points), BF16),
            pltpu.VMEM((3 * slots, cols, 2 * rank), BF16),
            pltpu.VMEM((3 * slots, cols, 2 * rank), BF16),
            pltpu.VMEM((slots, cols, rank), BF16),
            pltpu.VMEM((slots, cols, points), F32),
            pltpu.VMEM((slots, cols, points), F32),
            pltpu.VMEM((GROUP * rank, 4 * rank), BF16),
            pltpu.VMEM((groups * rank, 4 * rank), BF16),
            pltpu.VMEM((slots * rank, 2 * rank), BF16),
            pltpu.VMEM((2, GROUP, cols, 2 * rank), BF16),
            pltpu.VMEM((2, groups, cols, 2 * rank), BF16),
            pltpu.VMEM((2, GROUP, 8, 128), F32),
            pltpu.VMEM((2, groups, 8, 128), F32),
            dma((6,)),
            dma((slots,)),
            dma((2, 2, 2)),
            dma((2, 2, 2)),
            dma((2, GROUP - 1)),
            dma((2, GROUP - 1)),
            dma((2, groups - 1)),
            dma((2, groups - 1)),
            dma((2, GROUP - 1)),
            dma((2, GROUP - 1)),
            dma((2, groups - 1)),
            dma((2, groups - 1)),
        ],
        compiler_params=pltpu.CompilerParams(
            collective_id=0, has_side_effects=True, vmem_limit_bytes=60 * 1024 * 1024
        ),
    )(
        leaf_live,
        near_index.T,
        far_index.T,
        right_hand,
        near_tile,
        far_flat,
        leaf_basis,
        transfer_flat,
        up_flat,
        couple_flat,
    )


def solution(mesh):
    placed = (
        P("leaf", None, None),
        P("leaf"),
        P("leaf", None),
        P("leaf", None, None, None),
        P("leaf", None),
        P("leaf", None, None, None),
        P("leaf", None, None),
        P("leaf", None, None),
        P(),
        P(),
    )
    return jax.shard_map(
        on_device,
        mesh=mesh,
        in_specs=placed,
        out_specs=(P("leaf", None, None), P()),
        check_vma=False,
    )
```

```python
import functools
import jax
import jax.numpy as jnp
from jax import lax
from jax.experimental import pallas as pl
from jax.experimental.pallas import tpu as pltpu
from jax.sharding import PartitionSpec as P

epsilon = 1e-06
GROUP = 8
F32 = jnp.float32
BF16 = jnp.bfloat16


def dot(a, b):
    return jnp.dot(a, b, preferred_element_type=F32)


def dot_nt(a, b):
    return lax.dot_general(a, b, (((1,), (1,)), ((), ())), preferred_element_type=F32)


def to_columns(rows):
    return jnp.transpose(jnp.concatenate([rows] * 16, axis=0))


def kernel(
    n,
    live_ref,
    near_idx,
    far_idx,
    rhs_hbm,
    near_hbm,
    far_hbm,
    basis_hbm,
    transfer_hbm,
    up_hbm,
    couple_hbm,
    out_ref,
    hess_ref,
    rhs,
    near_t,
    far_t,
    basis,
    transfer,
    up,
    couple,
    own_0,
    own_1,
    full_0,
    full_1,
    mom_0,
    mom_1,
    local,
    w1,
    w2,
    weight_a,
    weight_b,
    twice,
    basis_t,
    spread_w,
    gat_a,
    gat_b,
    red_a,
    red_b,
    load_sem,
    near_sem,
    halo_send,
    halo_recv,
    a_send,
    a_recv,
    b_send,
    b_recv,
    ra_send,
    ra_recv,
    rb_send,
    rb_recv,
):
    slots, cols, points = rhs.shape
    own, full, mom = (own_0, own_1), (full_0, full_1), (mom_0, mom_1)
    rank = basis.shape[1]
    reach = (full_0.shape[0] - slots) // 2
    near_count = near_idx.shape[0]
    far_count = far_idx.shape[0]
    groups = n // GROUP
    levels = n.bit_length() - 1
    low = GROUP.bit_length() - 1
    me = lax.axis_index("leaf")
    j = me % GROUP
    base = me - j
    q = me // GROUP

    def load(hbm, vmem, k):
        return pltpu.make_async_copy(hbm, vmem, load_sem.at[k])

    loads = [
        load(rhs_hbm, rhs, 0),
        load(basis_hbm, basis, 1),
        load(transfer_hbm, transfer, 2),
        load(up_hbm, up, 3),
        load(couple_hbm, couple, 4),
        load(far_hbm, far_t, 5),
    ]
    for c in loads[:5]:
        c.start()

    def near_load(i):
        return pltpu.make_async_copy(near_hbm.at[i], near_t.at[i], near_sem.at[i])

    def start_near(i, carry):
        near_load(i).start()
        return carry

    lax.fori_loop(0, slots, start_near, 0)
    loads[5].start()

    for a in range(2):
        full[a][0:reach] = jnp.zeros((reach, cols, points), BF16)
        full[a][reach + slots : slots + 2 * reach] = jnp.zeros((reach, cols, points), BF16)
        mom[a][0:slots] = jnp.zeros((slots, cols, 2 * rank), BF16)
        mom[a][2 * slots : 3 * slots] = jnp.zeros((slots, cols, 2 * rank), BF16)

    barrier = pltpu.get_barrier_semaphore()

    def greet(dev):
        pl.semaphore_signal(barrier, inc=1, device_id=(dev,), device_id_type=pl.DeviceIdType.MESH)

    for k in range(1, GROUP):
        greet(base + (j + k) % GROUP)
    for k in range(1, groups):
        greet(((q + k) % groups) * GROUP + j)
    greet((me + 1) % n)
    greet((me + n - 1) % n)

    def remote(src, dst, send_sem, recv_sem, dev):
        return pltpu.make_async_remote_copy(
            src_ref=src,
            dst_ref=dst,
            send_sem=send_sem,
            recv_sem=recv_sem,
            device_id=(dev,),
            device_id_type=pl.DeviceIdType.MESH,
        )

    def copies_a(buf, s, r):
        return [
            remote(buf.at[j], buf.at[j], s.at[k - 1], r.at[k - 1], base + (j + k) % GROUP)
            for k in range(1, GROUP)
        ]

    def copies_b(buf, s, r):
        return [
            remote(buf.at[q], buf.at[q], s.at[k - 1], r.at[k - 1], ((q + k) % groups) * GROUP + j)
            for k in range(1, groups)
        ]

    def arrive_a(buf, s, r):
        for k in range(1, GROUP):
            src = (j + GROUP - k) % GROUP
            remote(buf.at[src], buf.at[src], s.at[k - 1], r.at[k - 1], base + src).wait_recv()

    def arrive_b(buf, s, r):
        for k in range(1, groups):
            src = (q + groups - k) % groups
            remote(
                buf.at[src], buf.at[src], s.at[k - 1], r.at[k - 1], src * GROUP + j
            ).wait_recv()

    def halo(a, kind):
        if kind == 0:
            up_src, up_dst = own[a].at[slots - reach : slots], full[a].at[0:reach]
            dn_src = own[a].at[0:reach]
            dn_dst = full[a].at[reach + slots : slots + 2 * reach]
        else:
            up_src, up_dst = mom[a].at[slots : 2 * slots], mom[a].at[0:slots]
            dn_src, dn_dst = mom[a].at[slots : 2 * slots], mom[a].at[2 * slots : 3 * slots]
        to_up = remote(up_src, up_dst, halo_send.at[a, kind, 0], halo_recv.at[a, kind, 0], (me + 1) % n)
        to_dn = remote(
            dn_src, dn_dst, halo_send.at[a, kind, 1], halo_recv.at[a, kind, 1], (me + n - 1) % n
        )
        return to_up, to_dn

    def halo_start(a, kind):
        to_up, to_dn = halo(a, kind)
        pl.when(me < n - 1)(to_up.start)
        pl.when(me > 0)(to_dn.start)

    def halo_arrive(a, kind):
        to_up, to_dn = halo(a, kind)
        pl.when(me > 0)(to_up.wait_recv)
        pl.when(me < n - 1)(to_dn.wait_recv)

    def halo_finish(a, kind):
        to_up, to_dn = halo(a, kind)
        pl.when(me < n - 1)(to_up.wait_send)
        pl.when(me > 0)(to_dn.wait_send)

    lane = lax.broadcasted_iota(jnp.int32, (cols, 2 * rank), 1)
    left_half = lane < rank

    def pair(x, y):
        return jnp.where(left_half, x, y)

    def halved(dup, parity):
        keep = (lane // rank) == parity
        return jnp.where(keep, dup, 0.0).astype(BF16)

    def moment_loop(a):
        def step(t, carry):
            i0 = t * 8
            got = []
            for u in range(8):
                got.append(dot(own[a][i0 + u], basis_t[i0 + u]).astype(BF16))
            for u in range(8):
                mom[a][slots + i0 + u] = got[u]
            return carry

        lax.fori_loop(0, slots // 8, step, 0)

    def transpose_basis(i, carry):
        b = basis[i]
        basis_t[i] = jnp.transpose(jnp.concatenate([b, b], axis=0))
        return carry

    def spread_weights(t, carry):
        got = []
        for u in range(4):
            i = t * 4 + u
            tr = transfer[pl.ds(pl.multiple_of(i * rank, rank), rank), :]
            got.append(
                lax.dot_general(
                    tr, basis[i], (((0,), (0,)), ((), ())), preferred_element_type=F32
                ).astype(BF16)
            )
        for u in range(4):
            spread_w[t * 4 + u, 0:rank] = basis[t * 4 + u]
            spread_w[t * 4 + u, rank : 2 * rank] = got[u]
        return carry

    def box_start(a):
        flat = jnp.concatenate(
            [pair(mom[a][slots + 2 * p], mom[a][slots + 2 * p + 1]) for p in range(slots // 2)],
            axis=1,
        )
        gat_a[a, j] = halved(dot(flat, twice[...]), j % 2)
        for c in copies_a(gat_a.at[a], a_send.at[a], a_recv.at[a]):
            c.start()

    def near_rows(a, rows, wait_tiles, src, shift):
        got = []
        first = me * slots - shift
        last = src[a].shape[0] - 1
        for i in rows:
            if wait_tiles:
                near_load(i).wait()
            v = jnp.concatenate(
                [src[a][jnp.clip(near_idx[k, i] - first, 0, last)] for k in range(near_count)], axis=1
            )
            got.append(dot(v, near_t[i].reshape(near_count * points, points)))
        for i, g in zip(rows, got):
            w2[i] = g

    def near_inner(a, lo, hi):
        def step(t, carry):
            i0 = lo + t * 4
            near_rows(a, [i0 + u for u in range(4)], a == 0, own, 0)
            return carry

        lax.fori_loop(0, (hi - lo) // 4, step, 0)

    def group_round(a):
        arrive_a(gat_a.at[a], a_send.at[a], a_recv.at[a])
        cat = jnp.concatenate(
            [gat_a[a, 2 * p] + gat_a[a, 2 * p + 1] for p in range(GROUP // 2)], axis=1
        )
        got = dot(cat, weight_a[...])
        gat_b[a, q] = halved(got[:, 2 * rank : 4 * rank], q % 2)
        for c in copies_b(gat_b.at[a], b_send.at[a], b_recv.at[a]):
            c.start()
        return got[:, : 2 * rank]

    def cross_round(a, part):
        arrive_b(gat_b.at[a], b_send.at[a], b_recv.at[a])
        cat = jnp.concatenate(
            [gat_b[a, 2 * p] + gat_b[a, 2 * p + 1] for p in range(groups // 2)], axis=1
        )
        total = part + dot(cat, weight_b[...])[:, : 2 * rank]
        return total.astype(BF16)

    def far_loop(a):
        first = me * slots - slots

        def source(i, f):
            return mom[a][jnp.clip(far_idx[f, i] - first, 0, 3 * slots - 1)]

        def step(t, carry):
            got = []
            for u in range(8):
                i = t * 8 + u
                v = jnp.concatenate(
                    [
                        pair(source(i, 2 * p), source(i, 2 * p + 1))
                        for p in range(far_count // 2)
                    ],
                    axis=1,
                )
                got.append(dot(v, far_t[i]).astype(BF16))
            for u in range(8):
                local[t * 8 + u, :, 0:rank] = got[u]
            return carry

        lax.fori_loop(0, slots // 8, step, 0)

    def spread(i, down):
        mask = live_ref[i].astype(F32)
        return (w2[i] + dot(pair(local[i], down), spread_w[i])) * mask

    def fold(x):
        return x[:, : points // 2] + x[:, points // 2 :]

    def pack(parts):
        wide = lax.broadcasted_iota(jnp.int32, (cols, 128), 1)
        total = jnp.zeros((cols, 128), F32)
        for k, p in enumerate(parts):
            total = total + jnp.where(wide == k, jnp.sum(p, axis=1, keepdims=True), 0.0)
        padded = jnp.concatenate([total, jnp.zeros((128 - cols, 128), F32)], axis=0)
        return jnp.transpose(padded)[:8]

    def reduce_first(t, rows):
        red_a[t, j] = rows
        for c in copies_a(red_a.at[t], ra_send.at[t], ra_recv.at[t]):
            c.start()

    def reduce_second(t):
        arrive_a(red_a.at[t], ra_send.at[t], ra_recv.at[t])
        total = red_a[t, 0]
        for k in range(1, GROUP):
            total = total + red_a[t, k]
        red_b[t, q] = total
        for c in copies_b(red_b.at[t], rb_send.at[t], rb_recv.at[t]):
            c.start()

    def reduce_third(t):
        arrive_b(red_b.at[t], rb_send.at[t], rb_recv.at[t])
        total = red_b[t, 0]
        for k in range(1, groups):
            total = total + red_b[t, k]
        return total

    loads[0].wait()

    def start_step(i, acc):
        s = rhs[i] * live_ref[i].astype(F32)
        rhs[i] = s
        v = s.astype(BF16)
        own[0][i] = v
        full[0][reach + i] = v
        return acc + fold(s * s)

    norm_part = lax.fori_loop(0, slots, start_step, jnp.zeros((cols, points // 2), F32))
    pl.semaphore_wait(barrier, GROUP - 1 + groups - 1 + 2)
    halo_start(0, 0)
    loads[1].wait()
    lax.fori_loop(0, slots, transpose_basis, 0)
    moment_loop(0)
    halo_start(0, 1)

    rowi = lax.broadcasted_iota(jnp.int32, (rank, 2 * rank), 0)
    coli = lax.broadcasted_iota(jnp.int32, (rank, 2 * rank), 1)
    eye_twice = jnp.where(rowi == coli % rank, 1.0, 0.0).astype(BF16)
    loads[2].wait()
    twice[...] = dot(transfer[...], eye_twice).astype(BF16)
    box_start(0)
    reduce_first(0, pack([norm_part]))

    loads[3].wait()
    loads[4].wait()

    def node_row(level, node):
        return pl.multiple_of((2 * n - 2 * (n >> level) + node) * rank, rank)

    def node_up(level, node, count):
        return up[pl.ds(node_row(level, node), count * rank), :]

    path = None
    couples = []
    for level in range(levels):
        c = couple[pl.ds(node_row(level, me >> level), rank), :]
        if path is None:
            r4 = lax.broadcasted_iota(jnp.int32, (4 * rank, rank), 0)
            c4 = lax.broadcasted_iota(jnp.int32, (4 * rank, rank), 1)
            path_pad = jnp.where((r4 % rank == c4) & (r4 < 2 * rank), 1.0, 0.0).astype(BF16)
        else:
            blank_rows = jnp.zeros((2 * rank, rank), BF16)
            path_pad = jnp.concatenate([path, path, blank_rows], axis=0)
        couples.append(dot_nt(c, path_pad))
        if level < levels - 1:
            u = node_up(level, me >> level, 1)
            path = u if path is None else dot(path, u).astype(BF16)

    def own_sibling(level, node):
        sibling = (me >> level) ^ 1
        f0 = jnp.where(sibling == node, 1.0, 0.0).astype(F32)
        f1 = jnp.where(sibling == node + 1, 1.0, 0.0).astype(F32)
        return jnp.concatenate([couples[level] * f0, couples[level] * f1], axis=0)

    wide_r = lax.broadcasted_iota(jnp.int32, (rank, 4 * rank), 0)
    wide_c = lax.broadcasted_iota(jnp.int32, (rank, 4 * rank), 1)
    root = jnp.where((wide_c >= 2 * rank) & (wide_r == wide_c % rank), 1.0, 0.0).astype(BF16)
    nodes = [root]
    for level in reversed(range(low)):
        below = []
        for m, x in enumerate(nodes):
            node = (base >> level) + 2 * m
            both = (dot(node_up(level, node, 2), x) + own_sibling(level, node)).astype(BF16)
            below.extend([both[:rank], both[rank:]])
        nodes = below
    for k, x in enumerate(nodes):
        weight_a[k * rank : (k + 1) * rank, :] = x
    nodes = [None]
    for level in reversed(range(low, levels)):
        below = []
        for m, x in enumerate(nodes):
            both = own_sibling(level, 2 * m)
            if x is not None:
                both = both + dot(node_up(level, 2 * m, 2), x)
            both = both.astype(BF16)
            below.extend([both[:rank], both[rank:]])
        nodes = below
    for k, x in enumerate(nodes):
        weight_b[k * rank : (k + 1) * rank, :] = x

    lax.fori_loop(0, slots // 4, spread_weights, 0)

    def operator_middle(a):
        split = reach + 4 * (a + 1)
        near_inner(a, reach, split)
        part = group_round(a)
        if a == 0:
            reduce_second(0)
        near_inner(a, split, slots - reach)
        halo_arrive(a, 0)
        near_rows(a, [0, 1, slots - 2, slots - 1], a == 0, full, reach)
        if a == 0:
            loads[5].wait()
        halo_arrive(a, 1)
        far_loop(a)
        return cross_round(a, part)

    down = operator_middle(0)
    norm_row = jnp.sqrt(reduce_third(0) + epsilon)
    inv_norm = to_columns(1.0 / norm_row)[:cols, 0:1]
    own_square = red_b[0, 0]
    for k in range(1, groups):
        own_square = own_square + red_b[0, k]

    def image_step(t, carry):
        got = [spread(t * 4 + u, down) * inv_norm for u in range(4)]
        for u in range(4):
            i = t * 4 + u
            v = got[u].astype(BF16)
            w1[i] = got[u]
            own[1][i] = v
            full[1][reach + i] = v
        return carry

    lax.fori_loop(0, slots // 4, image_step, 0)
    halo_start(1, 0)
    moment_loop(1)
    halo_start(1, 1)
    box_start(1)
    down = operator_middle(1)

    def gram_step(t, accs):
        got = [spread(t * 4 + u, down) for u in range(4)]
        for u in range(4):
            i = t * 4 + u
            z = got[u]
            w2[i] = z
            b = rhs[i] * inv_norm
            w = w1[i]
            accs = (
                accs[0] + fold(b * w),
                accs[1] + fold(w * w),
                accs[2] + fold(b * z),
                accs[3] + fold(w * z),
                accs[4] + fold(z * z),
            )
        return accs

    zero = jnp.zeros((cols, points // 2), F32)
    accs = lax.fori_loop(0, slots // 4, gram_step, (zero,) * 5)
    reduce_first(1, pack(accs))
    reduce_second(1)
    sums = reduce_third(1)

    norm = norm_row[0:1]
    unit = own_square[0:1] / (norm * norm)
    h, e, f, g, k2 = (sums[k : k + 1] for k in range(5))
    first_square = jnp.maximum(e - 2.0 * h * h + h * h * unit, 0.0)
    length = jnp.sqrt(first_square + epsilon)
    inv_l = 1.0 / length
    cross = (f - h * h) * inv_l
    inner = (g - h * e - h * f + h * h * h) * inv_l * inv_l
    image_square = (k2 - 2.0 * h * g + h * h * e) * inv_l * inv_l
    second_square = (
        image_square
        - 2.0 * cross * cross
        - 2.0 * inner * inner
        + cross * cross * unit
        + inner * inner * first_square * inv_l * inv_l
        + 2.0 * cross * inner * (h - h * unit) * inv_l
    )
    second = jnp.sqrt(jnp.maximum(second_square, 0.0) + epsilon)
    inv_s = 1.0 / second
    alpha = inv_l * inv_s
    beta = -(h + inner) * alpha
    gamma = (inner * h * inv_l - cross) * inv_s / norm
    blank = jnp.zeros((1, 128), F32)
    hess = jnp.concatenate([norm, h, length, cross, inner, second, blank, blank], axis=0)
    hess_ref[...] = hess[:6, :cols]
    coef = to_columns(jnp.concatenate([alpha, beta, gamma] + [blank] * 5, axis=0))
    ca, cb, cg = (coef[:cols, k : k + 1] for k in range(3))

    def out_step(i, carry):
        out_ref[i] = ca * w2[i] + cb * w1[i] + cg * rhs[i]
        return carry

    lax.fori_loop(0, slots, out_step, 0)

    for a in range(2):
        for c in copies_a(gat_a.at[a], a_send.at[a], a_recv.at[a]):
            c.wait_send()
        for c in copies_b(gat_b.at[a], b_send.at[a], b_recv.at[a]):
            c.wait_send()
        for c in copies_a(red_a.at[a], ra_send.at[a], ra_recv.at[a]):
            c.wait_send()
        for c in copies_b(red_b.at[a], rb_send.at[a], rb_recv.at[a]):
            c.wait_send()
        halo_finish(a, 0)
        halo_finish(a, 1)


def on_device(
    right_hand,
    leaf_live,
    near_index,
    near_tile,
    far_index,
    far_couple,
    leaf_basis,
    leaf_transfer,
    tree_up,
    tree_couple,
):
    n = lax.axis_size("leaf")
    slots, cols, points = right_hand.shape
    rank = leaf_basis.shape[1]
    far_count = far_index.shape[1]
    nodes = tree_up.shape[0]
    reach = 2
    groups = n // GROUP
    far_flat = far_couple.reshape(slots, far_count * rank, rank)
    transfer_flat = leaf_transfer.reshape(slots * rank, rank)
    up_flat = tree_up.reshape(nodes * rank, rank)
    couple_flat = tree_couple.reshape(nodes * rank, rank)
    smem = pl.BlockSpec(memory_space=pltpu.SMEM)
    anywhere = pl.BlockSpec(memory_space=pltpu.HBM)
    vmem = pl.BlockSpec(memory_space=pltpu.VMEM)
    dma = pltpu.SemaphoreType.DMA
    return pl.pallas_call(
        functools.partial(kernel, n),
        out_shape=(
            jax.ShapeDtypeStruct((slots, cols, points), F32),
            jax.ShapeDtypeStruct((6, cols), F32),
        ),
        in_specs=[smem] * 3 + [anywhere] * 7,
        out_specs=(vmem, vmem),
        scratch_shapes=[
            pltpu.VMEM((slots, cols, points), F32),
            pltpu.VMEM(near_tile.shape, BF16),
            pltpu.VMEM(far_flat.shape, BF16),
            pltpu.VMEM(leaf_basis.shape, BF16),
            pltpu.VMEM(transfer_flat.shape, BF16),
            pltpu.VMEM(up_flat.shape, BF16),
            pltpu.VMEM(couple_flat.shape, BF16),
            pltpu.VMEM((slots, cols, points), BF16),
            pltpu.VMEM((slots, cols, points), BF16),
            pltpu.VMEM((slots + 2 * reach, cols, points), BF16),
            pltpu.VMEM((slots + 2 * reach, cols, points), BF16),
            pltpu.VMEM((3 * slots, cols, 2 * rank), BF16),
            pltpu.VMEM((3 * slots, cols, 2 * rank), BF16),
            pltpu.VMEM((slots, cols, 2 * rank), BF16),
            pltpu.VMEM((slots, cols, points), F32),
            pltpu.VMEM((slots, cols, points), F32),
            pltpu.VMEM((GROUP * rank, 4 * rank), BF16),
            pltpu.VMEM((groups * rank, 4 * rank), BF16),
            pltpu.VMEM((slots * rank, 2 * rank), BF16),
            pltpu.VMEM((slots, points, 2 * rank), BF16),
            pltpu.VMEM((slots, 2 * rank, points), BF16),
            pltpu.VMEM((2, GROUP, cols, 2 * rank), BF16),
            pltpu.VMEM((2, groups, cols, 2 * rank), BF16),
            pltpu.VMEM((2, GROUP, 8, 128), F32),
            pltpu.VMEM((2, groups, 8, 128), F32),
            dma((6,)),
            dma((slots,)),
            dma((2, 2, 2)),
            dma((2, 2, 2)),
            dma((2, GROUP - 1)),
            dma((2, GROUP - 1)),
            dma((2, groups - 1)),
            dma((2, groups - 1)),
            dma((2, GROUP - 1)),
            dma((2, GROUP - 1)),
            dma((2, groups - 1)),
            dma((2, groups - 1)),
        ],
        compiler_params=pltpu.CompilerParams(
            collective_id=0, has_side_effects=True, vmem_limit_bytes=54016 * 1024
        ),
    )(
        leaf_live,
        near_index.T,
        far_index.T,
        right_hand,
        near_tile,
        far_flat,
        leaf_basis,
        transfer_flat,
        up_flat,
        couple_flat,
    )


def solution(mesh):
    placed = (
        P("leaf", None, None),
        P("leaf"),
        P("leaf", None),
        P("leaf", None, None, None),
        P("leaf", None),
        P("leaf", None, None, None),
        P("leaf", None, None),
        P("leaf", None, None),
        P(),
        P(),
    )
    return jax.shard_map(
        on_device,
        mesh=mesh,
        in_specs=placed,
        out_specs=(P("leaf", None, None), P()),
        check_vma=False,
    )
```

```python
import functools
import jax
import jax.numpy as jnp
from jax import lax
from jax.experimental import pallas as pl
from jax.experimental.pallas import tpu as pltpu
from jax.sharding import PartitionSpec as P

epsilon = 1e-06
GROUP = 8
F32 = jnp.float32
BF16 = jnp.bfloat16


def dot(a, b):
    return jnp.dot(a, b, preferred_element_type=F32)


def dot_nt(a, b):
    return lax.dot_general(a, b, (((1,), (1,)), ((), ())), preferred_element_type=F32)


def to_columns(rows):
    return jnp.transpose(jnp.concatenate([rows] * 16, axis=0))


def kernel(
    n,
    live_ref,
    near_idx,
    far_idx,
    rhs_hbm,
    near_hbm,
    far_hbm,
    basis_hbm,
    transfer_hbm,
    up_hbm,
    couple_hbm,
    out_ref,
    hess_ref,
    rhs,
    near_t,
    far_t,
    basis,
    transfer,
    up,
    couple,
    own_0,
    own_1,
    full_0,
    full_1,
    mom_0,
    mom_1,
    local,
    w1,
    w2,
    weight_a,
    weight_b,
    twice,
    basis_t,
    spread_w,
    far_four,
    gat_a,
    gat_b,
    red_a,
    red_b,
    load_sem,
    near_sem,
    halo_send,
    halo_recv,
    a_send,
    a_recv,
    b_send,
    b_recv,
    ra_send,
    ra_recv,
    rb_send,
    rb_recv,
):
    slots, cols, points = rhs.shape
    own, full, mom = (own_0, own_1), (full_0, full_1), (mom_0, mom_1)
    rank = basis.shape[1]
    reach = (full_0.shape[0] - slots) // 2
    near_count = near_idx.shape[0]
    far_count = far_idx.shape[0]
    groups = n // GROUP
    levels = n.bit_length() - 1
    low = GROUP.bit_length() - 1
    me = lax.axis_index("leaf")
    j = me % GROUP
    base = me - j
    q = me // GROUP

    def load(hbm, vmem, k):
        return pltpu.make_async_copy(hbm, vmem, load_sem.at[k])

    loads = [
        load(rhs_hbm, rhs, 0),
        load(basis_hbm, basis, 1),
        load(transfer_hbm, transfer, 2),
        load(up_hbm, up, 3),
        load(couple_hbm, couple, 4),
        load(far_hbm, far_t, 5),
    ]
    for c in loads[:5]:
        c.start()

    def near_load(i):
        return pltpu.make_async_copy(near_hbm.at[i], near_t.at[i], near_sem.at[i])

    def start_near(i, carry):
        near_load(i).start()
        return carry

    lax.fori_loop(0, slots, start_near, 0)
    loads[5].start()

    for a in range(2):
        full[a][0:reach] = jnp.zeros((reach, cols, points), BF16)
        full[a][reach + slots : slots + 2 * reach] = jnp.zeros((reach, cols, points), BF16)
        mom[a][0:slots] = jnp.zeros((slots, cols, 2 * rank), BF16)
        mom[a][2 * slots : 3 * slots] = jnp.zeros((slots, cols, 2 * rank), BF16)

    barrier = pltpu.get_barrier_semaphore()

    def greet(dev):
        pl.semaphore_signal(barrier, inc=1, device_id=(dev,), device_id_type=pl.DeviceIdType.MESH)

    for k in range(1, GROUP):
        greet(base + (j + k) % GROUP)
    for k in range(1, groups):
        greet(((q + k) % groups) * GROUP + j)
    greet((me + 1) % n)
    greet((me + n - 1) % n)

    def remote(src, dst, send_sem, recv_sem, dev):
        return pltpu.make_async_remote_copy(
            src_ref=src,
            dst_ref=dst,
            send_sem=send_sem,
            recv_sem=recv_sem,
            device_id=(dev,),
            device_id_type=pl.DeviceIdType.MESH,
        )

    def copies_a(buf, s, r):
        return [
            remote(buf.at[j], buf.at[j], s.at[k - 1], r.at[k - 1], base + (j + k) % GROUP)
            for k in range(1, GROUP)
        ]

    def copies_b(buf, s, r):
        return [
            remote(buf.at[q], buf.at[q], s.at[k - 1], r.at[k - 1], ((q + k) % groups) * GROUP + j)
            for k in range(1, groups)
        ]

    def arrive_a(buf, s, r):
        for k in range(1, GROUP):
            src = (j + GROUP - k) % GROUP
            remote(buf.at[src], buf.at[src], s.at[k - 1], r.at[k - 1], base + src).wait_recv()

    def arrive_b(buf, s, r):
        for k in range(1, groups):
            src = (q + groups - k) % groups
            remote(
                buf.at[src], buf.at[src], s.at[k - 1], r.at[k - 1], src * GROUP + j
            ).wait_recv()

    def halo(a, kind):
        if kind == 0:
            up_src, up_dst = own[a].at[slots - reach : slots], full[a].at[0:reach]
            dn_src = own[a].at[0:reach]
            dn_dst = full[a].at[reach + slots : slots + 2 * reach]
        else:
            up_src, up_dst = mom[a].at[slots : 2 * slots], mom[a].at[0:slots]
            dn_src, dn_dst = mom[a].at[slots : 2 * slots], mom[a].at[2 * slots : 3 * slots]
        to_up = remote(up_src, up_dst, halo_send.at[a, kind, 0], halo_recv.at[a, kind, 0], (me + 1) % n)
        to_dn = remote(
            dn_src, dn_dst, halo_send.at[a, kind, 1], halo_recv.at[a, kind, 1], (me + n - 1) % n
        )
        return to_up, to_dn

    def halo_start(a, kind):
        to_up, to_dn = halo(a, kind)
        pl.when(me < n - 1)(to_up.start)
        pl.when(me > 0)(to_dn.start)

    def halo_arrive(a, kind):
        to_up, to_dn = halo(a, kind)
        pl.when(me > 0)(to_up.wait_recv)
        pl.when(me < n - 1)(to_dn.wait_recv)

    def halo_finish(a, kind):
        to_up, to_dn = halo(a, kind)
        pl.when(me < n - 1)(to_up.wait_send)
        pl.when(me > 0)(to_dn.wait_send)

    lane = lax.broadcasted_iota(jnp.int32, (cols, 2 * rank), 1)
    left_half = lane < rank

    def pair(x, y):
        return jnp.where(left_half, x, y)

    def halved(dup, parity):
        keep = (lane // rank) == parity
        return jnp.where(keep, dup, 0.0).astype(BF16)

    def moment_loop(a):
        def step(t, carry):
            got = []
            for u in range(4):
                p = t * 4 + u
                v = jnp.concatenate([own[a][2 * p], own[a][2 * p + 1]], axis=0)
                got.append(dot(v, basis_t[p]).astype(BF16))
            for u in range(4):
                p = t * 4 + u
                mom[a][slots + 2 * p] = got[u][:cols, : 2 * rank]
                mom[a][slots + 2 * p + 1] = got[u][cols:, 2 * rank :]
            return carry

        lax.fori_loop(0, slots // 8, step, 0)

    def transpose_basis(p, carry):
        b0, b1 = basis[2 * p], basis[2 * p + 1]
        basis_t[p] = jnp.transpose(jnp.concatenate([b0, b0, b1, b1], axis=0))
        return carry

    def pack_far(t, carry):
        far_four[t] = jnp.concatenate([far_t[t * 4 + u] for u in range(4)], axis=1)
        return carry

    def spread_weights(t, carry):
        got = []
        for u in range(4):
            i = t * 4 + u
            tr = transfer[pl.ds(pl.multiple_of(i * rank, rank), rank), :]
            got.append(
                lax.dot_general(
                    tr, basis[i], (((0,), (0,)), ((), ())), preferred_element_type=F32
                ).astype(BF16)
            )
        for u in range(4):
            halves = (basis[t * 4 + u], got[u])
            spread_w[t * 4 + u, 0:rank] = halves[u % 2]
            spread_w[t * 4 + u, rank : 2 * rank] = halves[1 - u % 2]
        return carry

    def box_start(a):
        flat = jnp.concatenate(
            [pair(mom[a][slots + 2 * p], mom[a][slots + 2 * p + 1]) for p in range(slots // 2)],
            axis=1,
        )
        gat_a[a, j] = halved(dot(flat, twice[...]), j % 2)
        for c in copies_a(gat_a.at[a], a_send.at[a], a_recv.at[a]):
            c.start()

    def near_rows(a, rows, wait_tiles, src, shift):
        got = []
        first = me * slots - shift
        last = src[a].shape[0] - 1
        for i in rows:
            if wait_tiles:
                near_load(i).wait()
            v = jnp.concatenate(
                [src[a][jnp.clip(near_idx[k, i] - first, 0, last)] for k in range(near_count)], axis=1
            )
            got.append(dot(v, near_t[i].reshape(near_count * points, points)))
        for i, g in zip(rows, got):
            w2[i] = g

    def near_inner(a, lo, hi):
        def step(t, carry):
            i0 = lo + t * 4
            near_rows(a, [i0 + u for u in range(4)], a == 0, own, 0)
            return carry

        lax.fori_loop(0, (hi - lo) // 4, step, 0)

    def group_round(a):
        arrive_a(gat_a.at[a], a_send.at[a], a_recv.at[a])
        cat = jnp.concatenate(
            [gat_a[a, 2 * p] + gat_a[a, 2 * p + 1] for p in range(GROUP // 2)], axis=1
        )
        got = dot(cat, weight_a[...])
        gat_b[a, q] = halved(got[:, 2 * rank : 4 * rank], q % 2)
        for c in copies_b(gat_b.at[a], b_send.at[a], b_recv.at[a]):
            c.start()
        return got[:, : 2 * rank]

    def cross_round(a, part):
        arrive_b(gat_b.at[a], b_send.at[a], b_recv.at[a])
        cat = jnp.concatenate(
            [gat_b[a, 2 * p] + gat_b[a, 2 * p + 1] for p in range(groups // 2)], axis=1
        )
        total = part + dot(cat, weight_b[...])[:, : 2 * rank]
        return total.astype(BF16)

    def far_loop(a):
        first = me * slots - slots

        def source(i, f):
            return mom[a][jnp.clip(far_idx[f, i] - first, 0, 3 * slots - 1)]

        def step(t, carry):
            stack = []
            for u in range(4):
                i = t * 4 + u
                stack.append(
                    jnp.concatenate(
                        [
                            pair(source(i, 2 * p), source(i, 2 * p + 1))
                            for p in range(far_count // 2)
                        ],
                        axis=1,
                    )
                )
            got = dot(jnp.concatenate(stack, axis=0), far_four[t]).astype(BF16)
            for u in range(4):
                k = (u // 2) * 2 * rank
                local[t * 4 + u] = got[u * cols : (u + 1) * cols, k : k + 2 * rank]
            return carry

        lax.fori_loop(0, slots // 4, step, 0)

    def spread(i, odd, down):
        mask = live_ref[i].astype(F32)
        both = pair(down, local[i]) if odd else pair(local[i], down)
        return (w2[i] + dot(both, spread_w[i])) * mask

    def fold(x):
        return x[:, : points // 2] + x[:, points // 2 :]

    def pack(parts):
        wide = lax.broadcasted_iota(jnp.int32, (cols, 128), 1)
        total = jnp.zeros((cols, 128), F32)
        for k, p in enumerate(parts):
            total = total + jnp.where(wide == k, jnp.sum(p, axis=1, keepdims=True), 0.0)
        padded = jnp.concatenate([total, jnp.zeros((128 - cols, 128), F32)], axis=0)
        return jnp.transpose(padded)[:8]

    def reduce_first(t, rows):
        red_a[t, j] = rows
        for c in copies_a(red_a.at[t], ra_send.at[t], ra_recv.at[t]):
            c.start()

    def reduce_second(t):
        arrive_a(red_a.at[t], ra_send.at[t], ra_recv.at[t])
        total = red_a[t, 0]
        for k in range(1, GROUP):
            total = total + red_a[t, k]
        red_b[t, q] = total
        for c in copies_b(red_b.at[t], rb_send.at[t], rb_recv.at[t]):
            c.start()

    def reduce_third(t):
        arrive_b(red_b.at[t], rb_send.at[t], rb_recv.at[t])
        total = red_b[t, 0]
        for k in range(1, groups):
            total = total + red_b[t, k]
        return total

    loads[0].wait()

    def start_step(i, acc):
        s = rhs[i] * live_ref[i].astype(F32)
        rhs[i] = s
        v = s.astype(BF16)
        own[0][i] = v
        full[0][reach + i] = v
        return acc + fold(s * s)

    norm_part = lax.fori_loop(0, slots, start_step, jnp.zeros((cols, points // 2), F32))
    pl.semaphore_wait(barrier, GROUP - 1 + groups - 1 + 2)
    halo_start(0, 0)
    loads[1].wait()
    lax.fori_loop(0, slots // 2, transpose_basis, 0)
    moment_loop(0)
    halo_start(0, 1)

    rowi = lax.broadcasted_iota(jnp.int32, (rank, 2 * rank), 0)
    coli = lax.broadcasted_iota(jnp.int32, (rank, 2 * rank), 1)
    eye_twice = jnp.where(rowi == coli % rank, 1.0, 0.0).astype(BF16)
    loads[2].wait()
    twice[...] = dot(transfer[...], eye_twice).astype(BF16)
    box_start(0)
    reduce_first(0, pack([norm_part]))

    loads[3].wait()
    loads[4].wait()

    def node_row(level, node):
        return pl.multiple_of((2 * n - 2 * (n >> level) + node) * rank, rank)

    def node_up(level, node, count):
        return up[pl.ds(node_row(level, node), count * rank), :]

    path = None
    couples = []
    for level in range(levels):
        c = couple[pl.ds(node_row(level, me >> level), rank), :]
        if path is None:
            r4 = lax.broadcasted_iota(jnp.int32, (4 * rank, rank), 0)
            c4 = lax.broadcasted_iota(jnp.int32, (4 * rank, rank), 1)
            path_pad = jnp.where((r4 % rank == c4) & (r4 < 2 * rank), 1.0, 0.0).astype(BF16)
        else:
            blank_rows = jnp.zeros((2 * rank, rank), BF16)
            path_pad = jnp.concatenate([path, path, blank_rows], axis=0)
        couples.append(dot_nt(c, path_pad))
        if level < levels - 1:
            u = node_up(level, me >> level, 1)
            path = u if path is None else dot(path, u).astype(BF16)

    def own_sibling(level, node):
        sibling = (me >> level) ^ 1
        f0 = jnp.where(sibling == node, 1.0, 0.0).astype(F32)
        f1 = jnp.where(sibling == node + 1, 1.0, 0.0).astype(F32)
        return jnp.concatenate([couples[level] * f0, couples[level] * f1], axis=0)

    wide_r = lax.broadcasted_iota(jnp.int32, (rank, 4 * rank), 0)
    wide_c = lax.broadcasted_iota(jnp.int32, (rank, 4 * rank), 1)
    root = jnp.where((wide_c >= 2 * rank) & (wide_r == wide_c % rank), 1.0, 0.0).astype(BF16)
    nodes = [root]
    for level in reversed(range(low)):
        below = []
        for m, x in enumerate(nodes):
            node = (base >> level) + 2 * m
            both = (dot(node_up(level, node, 2), x) + own_sibling(level, node)).astype(BF16)
            below.extend([both[:rank], both[rank:]])
        nodes = below
    for k, x in enumerate(nodes):
        weight_a[k * rank : (k + 1) * rank, :] = x
    nodes = [None]
    for level in reversed(range(low, levels)):
        below = []
        for m, x in enumerate(nodes):
            both = own_sibling(level, 2 * m)
            if x is not None:
                both = both + dot(node_up(level, 2 * m, 2), x)
            both = both.astype(BF16)
            below.extend([both[:rank], both[rank:]])
        nodes = below
    for k, x in enumerate(nodes):
        weight_b[k * rank : (k + 1) * rank, :] = x

    lax.fori_loop(0, slots // 4, spread_weights, 0)

    def operator_middle(a):
        split = reach + 4 * (a + 1)
        near_inner(a, reach, split)
        part = group_round(a)
        if a == 0:
            reduce_second(0)
        near_inner(a, split, slots - reach)
        halo_arrive(a, 0)
        near_rows(a, [0, 1, slots - 2, slots - 1], a == 0, full, reach)
        if a == 0:
            loads[5].wait()
            lax.fori_loop(0, slots // 4, pack_far, 0)
        halo_arrive(a, 1)
        far_loop(a)
        return cross_round(a, part)

    down = operator_middle(0)
    norm_row = jnp.sqrt(reduce_third(0) + epsilon)
    inv_norm = to_columns(1.0 / norm_row)[:cols, 0:1]
    own_square = red_b[0, 0]
    for k in range(1, groups):
        own_square = own_square + red_b[0, k]

    def image_step(t, carry):
        got = [spread(t * 4 + u, u % 2, down) * inv_norm for u in range(4)]
        for u in range(4):
            i = t * 4 + u
            v = got[u].astype(BF16)
            w1[i] = got[u]
            own[1][i] = v
            full[1][reach + i] = v
        return carry

    lax.fori_loop(0, slots // 4, image_step, 0)
    halo_start(1, 0)
    moment_loop(1)
    halo_start(1, 1)
    box_start(1)
    down = operator_middle(1)

    def gram_step(t, accs):
        got = [spread(t * 4 + u, u % 2, down) for u in range(4)]
        for u in range(4):
            i = t * 4 + u
            z = got[u]
            w2[i] = z
            b = rhs[i] * inv_norm
            w = w1[i]
            accs = (
                accs[0] + fold(b * w),
                accs[1] + fold(w * w),
                accs[2] + fold(b * z),
                accs[3] + fold(w * z),
                accs[4] + fold(z * z),
            )
        return accs

    zero = jnp.zeros((cols, points // 2), F32)
    accs = lax.fori_loop(0, slots // 4, gram_step, (zero,) * 5)
    reduce_first(1, pack(accs))
    reduce_second(1)
    sums = reduce_third(1)

    norm = norm_row[0:1]
    unit = own_square[0:1] / (norm * norm)
    h, e, f, g, k2 = (sums[k : k + 1] for k in range(5))
    first_square = jnp.maximum(e - 2.0 * h * h + h * h * unit, 0.0)
    length = jnp.sqrt(first_square + epsilon)
    inv_l = 1.0 / length
    cross = (f - h * h) * inv_l
    inner = (g - h * e - h * f + h * h * h) * inv_l * inv_l
    image_square = (k2 - 2.0 * h * g + h * h * e) * inv_l * inv_l
    second_square = (
        image_square
        - 2.0 * cross * cross
        - 2.0 * inner * inner
        + cross * cross * unit
        + inner * inner * first_square * inv_l * inv_l
        + 2.0 * cross * inner * (h - h * unit) * inv_l
    )
    second = jnp.sqrt(jnp.maximum(second_square, 0.0) + epsilon)
    inv_s = 1.0 / second
    alpha = inv_l * inv_s
    beta = -(h + inner) * alpha
    gamma = (inner * h * inv_l - cross) * inv_s / norm
    blank = jnp.zeros((1, 128), F32)
    hess = jnp.concatenate([norm, h, length, cross, inner, second, blank, blank], axis=0)
    hess_ref[...] = hess[:6, :cols]
    coef = to_columns(jnp.concatenate([alpha, beta, gamma] + [blank] * 5, axis=0))
    ca, cb, cg = (coef[:cols, k : k + 1] for k in range(3))

    def out_step(i, carry):
        out_ref[i] = ca * w2[i] + cb * w1[i] + cg * rhs[i]
        return carry

    lax.fori_loop(0, slots, out_step, 0)

    for a in range(2):
        for c in copies_a(gat_a.at[a], a_send.at[a], a_recv.at[a]):
            c.wait_send()
        for c in copies_b(gat_b.at[a], b_send.at[a], b_recv.at[a]):
            c.wait_send()
        for c in copies_a(red_a.at[a], ra_send.at[a], ra_recv.at[a]):
            c.wait_send()
        for c in copies_b(red_b.at[a], rb_send.at[a], rb_recv.at[a]):
            c.wait_send()
        halo_finish(a, 0)
        halo_finish(a, 1)


def on_device(
    right_hand,
    leaf_live,
    near_index,
    near_tile,
    far_index,
    far_couple,
    leaf_basis,
    leaf_transfer,
    tree_up,
    tree_couple,
):
    n = lax.axis_size("leaf")
    slots, cols, points = right_hand.shape
    rank = leaf_basis.shape[1]
    far_count = far_index.shape[1]
    nodes = tree_up.shape[0]
    reach = 2
    groups = n // GROUP
    far_flat = far_couple.reshape(slots, far_count * rank, rank)
    transfer_flat = leaf_transfer.reshape(slots * rank, rank)
    up_flat = tree_up.reshape(nodes * rank, rank)
    couple_flat = tree_couple.reshape(nodes * rank, rank)
    smem = pl.BlockSpec(memory_space=pltpu.SMEM)
    anywhere = pl.BlockSpec(memory_space=pltpu.HBM)
    vmem = pl.BlockSpec(memory_space=pltpu.VMEM)
    dma = pltpu.SemaphoreType.DMA
    return pl.pallas_call(
        functools.partial(kernel, n),
        out_shape=(
            jax.ShapeDtypeStruct((slots, cols, points), F32),
            jax.ShapeDtypeStruct((6, cols), F32),
        ),
        in_specs=[smem] * 3 + [anywhere] * 7,
        out_specs=(vmem, vmem),
        scratch_shapes=[
            pltpu.VMEM((slots, cols, points), F32),
            pltpu.VMEM(near_tile.shape, BF16),
            pltpu.VMEM(far_flat.shape, BF16),
            pltpu.VMEM(leaf_basis.shape, BF16),
            pltpu.VMEM(transfer_flat.shape, BF16),
            pltpu.VMEM(up_flat.shape, BF16),
            pltpu.VMEM(couple_flat.shape, BF16),
            pltpu.VMEM((slots, cols, points), BF16),
            pltpu.VMEM((slots, cols, points), BF16),
            pltpu.VMEM((slots + 2 * reach, cols, points), BF16),
            pltpu.VMEM((slots + 2 * reach, cols, points), BF16),
            pltpu.VMEM((3 * slots, cols, 2 * rank), BF16),
            pltpu.VMEM((3 * slots, cols, 2 * rank), BF16),
            pltpu.VMEM((slots, cols, 2 * rank), BF16),
            pltpu.VMEM((slots, cols, points), F32),
            pltpu.VMEM((slots, cols, points), F32),
            pltpu.VMEM((GROUP * rank, 4 * rank), BF16),
            pltpu.VMEM((groups * rank, 4 * rank), BF16),
            pltpu.VMEM((slots * rank, 2 * rank), BF16),
            pltpu.VMEM((slots // 2, points, 4 * rank), BF16),
            pltpu.VMEM((slots, 2 * rank, points), BF16),
            pltpu.VMEM((slots // 4, far_count * rank, 4 * rank), BF16),
            pltpu.VMEM((2, GROUP, cols, 2 * rank), BF16),
            pltpu.VMEM((2, groups, cols, 2 * rank), BF16),
            pltpu.VMEM((2, GROUP, 8, 128), F32),
            pltpu.VMEM((2, groups, 8, 128), F32),
            dma((6,)),
            dma((slots,)),
            dma((2, 2, 2)),
            dma((2, 2, 2)),
            dma((2, GROUP - 1)),
            dma((2, GROUP - 1)),
            dma((2, groups - 1)),
            dma((2, groups - 1)),
            dma((2, GROUP - 1)),
            dma((2, GROUP - 1)),
            dma((2, groups - 1)),
            dma((2, groups - 1)),
        ],
        compiler_params=pltpu.CompilerParams(
            collective_id=0, has_side_effects=True, vmem_limit_bytes=60 * 1024 * 1024
        ),
    )(
        leaf_live,
        near_index.T,
        far_index.T,
        right_hand,
        near_tile,
        far_flat,
        leaf_basis,
        transfer_flat,
        up_flat,
        couple_flat,
    )


def solution(mesh):
    placed = (
        P("leaf", None, None),
        P("leaf"),
        P("leaf", None),
        P("leaf", None, None, None),
        P("leaf", None),
        P("leaf", None, None, None),
        P("leaf", None, None),
        P("leaf", None, None),
        P(),
        P(),
    )
    return jax.shard_map(
        on_device,
        mesh=mesh,
        in_specs=placed,
        out_specs=(P("leaf", None, None), P()),
        check_vma=False,
    )
```

```python
import functools
import jax
import jax.numpy as jnp
from jax import lax
from jax.experimental import pallas as pl
from jax.experimental.pallas import tpu as pltpu
from jax.sharding import PartitionSpec as P

epsilon = 1e-06
GROUP = 8
F32 = jnp.float32
BF16 = jnp.bfloat16


def dot(a, b):
    return jnp.dot(a, b, preferred_element_type=F32)


def dot_nt(a, b):
    return lax.dot_general(a, b, (((1,), (1,)), ((), ())), preferred_element_type=F32)


def to_columns(rows):
    return jnp.transpose(jnp.concatenate([rows] * 16, axis=0))


def kernel(
    n,
    live_ref,
    near_idx,
    far_idx,
    rhs_hbm,
    near_hbm,
    far_hbm,
    basis_hbm,
    transfer_hbm,
    up_hbm,
    couple_hbm,
    out_ref,
    hess_ref,
    rhs,
    near_t,
    far_t,
    basis,
    transfer,
    up,
    couple,
    own_0,
    own_1,
    full_0,
    full_1,
    mom_0,
    mom_1,
    local,
    w1,
    w2,
    weight_a,
    weight_b,
    twice,
    basis_t,
    spread_w,
    gat_a,
    gat_b,
    red_a,
    red_b,
    load_sem,
    near_sem,
    halo_send,
    halo_recv,
    a_send,
    a_recv,
    b_send,
    b_recv,
    ra_send,
    ra_recv,
    rb_send,
    rb_recv,
):
    slots, cols, points = rhs.shape
    own, full, mom = (own_0, own_1), (full_0, full_1), (mom_0, mom_1)
    rank = basis.shape[1]
    reach = (full_0.shape[0] - slots) // 2
    near_count = near_idx.shape[0]
    far_count = far_idx.shape[0]
    groups = n // GROUP
    levels = n.bit_length() - 1
    low = GROUP.bit_length() - 1
    me = lax.axis_index("leaf")
    j = me % GROUP
    base = me - j
    q = me // GROUP

    def load(hbm, vmem, k):
        return pltpu.make_async_copy(hbm, vmem, load_sem.at[k])

    loads = [
        load(rhs_hbm, rhs, 0),
        load(basis_hbm, basis, 1),
        load(transfer_hbm, transfer, 2),
        load(up_hbm, up, 3),
        load(couple_hbm, couple, 4),
        load(far_hbm, far_t, 5),
    ]
    for c in loads[:5]:
        c.start()

    def near_load(i):
        return pltpu.make_async_copy(near_hbm.at[i], near_t.at[i], near_sem.at[i])

    def start_near(i, carry):
        near_load(i).start()
        return carry

    lax.fori_loop(0, slots, start_near, 0)
    loads[5].start()

    for a in range(2):
        full[a][0:reach] = jnp.zeros((reach, cols, points), BF16)
        full[a][reach + slots : slots + 2 * reach] = jnp.zeros((reach, cols, points), BF16)
        mom[a][0:slots] = jnp.zeros((slots, cols, 2 * rank), BF16)
        mom[a][2 * slots : 3 * slots] = jnp.zeros((slots, cols, 2 * rank), BF16)

    barrier = pltpu.get_barrier_semaphore()

    def greet(dev):
        pl.semaphore_signal(barrier, inc=1, device_id=(dev,), device_id_type=pl.DeviceIdType.MESH)

    for k in range(1, GROUP):
        greet(base + (j + k) % GROUP)
    for k in range(1, groups):
        greet(((q + k) % groups) * GROUP + j)
    greet((me + 1) % n)
    greet((me + n - 1) % n)

    def remote(src, dst, send_sem, recv_sem, dev):
        return pltpu.make_async_remote_copy(
            src_ref=src,
            dst_ref=dst,
            send_sem=send_sem,
            recv_sem=recv_sem,
            device_id=(dev,),
            device_id_type=pl.DeviceIdType.MESH,
        )

    def copies_a(buf, s, r):
        return [
            remote(buf.at[j], buf.at[j], s.at[k - 1], r.at[k - 1], base + (j + k) % GROUP)
            for k in range(1, GROUP)
        ]

    def copies_b(buf, s, r):
        return [
            remote(buf.at[q], buf.at[q], s.at[k - 1], r.at[k - 1], ((q + k) % groups) * GROUP + j)
            for k in range(1, groups)
        ]

    def arrive_a(buf, s, r):
        for k in range(1, GROUP):
            src = (j + GROUP - k) % GROUP
            remote(buf.at[src], buf.at[src], s.at[k - 1], r.at[k - 1], base + src).wait_recv()

    def arrive_b(buf, s, r):
        for k in range(1, groups):
            src = (q + groups - k) % groups
            remote(
                buf.at[src], buf.at[src], s.at[k - 1], r.at[k - 1], src * GROUP + j
            ).wait_recv()

    def halo(a, kind):
        if kind == 0:
            up_src, up_dst = own[a].at[slots - reach : slots], full[a].at[0:reach]
            dn_src = own[a].at[0:reach]
            dn_dst = full[a].at[reach + slots : slots + 2 * reach]
        else:
            up_src, up_dst = mom[a].at[slots : 2 * slots], mom[a].at[0:slots]
            dn_src, dn_dst = mom[a].at[slots : 2 * slots], mom[a].at[2 * slots : 3 * slots]
        to_up = remote(up_src, up_dst, halo_send.at[a, kind, 0], halo_recv.at[a, kind, 0], (me + 1) % n)
        to_dn = remote(
            dn_src, dn_dst, halo_send.at[a, kind, 1], halo_recv.at[a, kind, 1], (me + n - 1) % n
        )
        return to_up, to_dn

    def halo_start(a, kind):
        to_up, to_dn = halo(a, kind)
        pl.when(me < n - 1)(to_up.start)
        pl.when(me > 0)(to_dn.start)

    def halo_arrive(a, kind):
        to_up, to_dn = halo(a, kind)
        pl.when(me > 0)(to_up.wait_recv)
        pl.when(me < n - 1)(to_dn.wait_recv)

    def halo_finish(a, kind):
        to_up, to_dn = halo(a, kind)
        pl.when(me < n - 1)(to_up.wait_send)
        pl.when(me > 0)(to_dn.wait_send)

    lane = lax.broadcasted_iota(jnp.int32, (cols, 2 * rank), 1)
    left_half = lane < rank

    def pair(x, y):
        return jnp.where(left_half, x, y)

    def halved(dup, parity):
        keep = (lane // rank) == parity
        return jnp.where(keep, dup, 0.0).astype(BF16)

    def moment_loop(a):
        def step(t, carry):
            i0 = t * 8
            got = []
            for u in range(8):
                got.append(dot(own[a][i0 + u], basis_t[i0 + u]).astype(BF16))
            for u in range(8):
                mom[a][slots + i0 + u] = got[u]
            return carry

        lax.fori_loop(0, slots // 8, step, 0)

    def transpose_basis(i, carry):
        b = basis[i]
        basis_t[i] = jnp.transpose(jnp.concatenate([b, b], axis=0))
        return carry

    def spread_weights(t, carry):
        got = []
        for u in range(4):
            i = t * 4 + u
            tr = transfer[pl.ds(pl.multiple_of(i * rank, rank), rank), :]
            got.append(
                lax.dot_general(
                    tr, basis[i], (((0,), (0,)), ((), ())), preferred_element_type=F32
                ).astype(BF16)
            )
        for u in range(4):
            spread_w[t * 4 + u, 0:rank] = basis[t * 4 + u]
            spread_w[t * 4 + u, rank : 2 * rank] = got[u]
        return carry

    def box_start(a):
        flat = jnp.concatenate(
            [pair(mom[a][slots + 2 * p], mom[a][slots + 2 * p + 1]) for p in range(slots // 2)],
            axis=1,
        )
        gat_a[a, j] = halved(dot(flat, twice[...]), j % 2)
        for c in copies_a(gat_a.at[a], a_send.at[a], a_recv.at[a]):
            c.start()

    def near_rows(a, rows, wait_tiles, src, shift):
        got = []
        first = me * slots - shift
        last = src[a].shape[0] - 1
        for i in rows:
            if wait_tiles:
                near_load(i).wait()
            v = jnp.concatenate(
                [src[a][jnp.clip(near_idx[k, i] - first, 0, last)] for k in range(near_count)], axis=1
            )
            got.append(dot(v, near_t[i].reshape(near_count * points, points)))
        for i, g in zip(rows, got):
            w2[i] = g

    def near_inner(a, lo, hi):
        def step(t, carry):
            i0 = lo + t * 4
            near_rows(a, [i0 + u for u in range(4)], a == 0, own, 0)
            return carry

        lax.fori_loop(0, (hi - lo) // 4, step, 0)

    def group_round(a):
        arrive_a(gat_a.at[a], a_send.at[a], a_recv.at[a])
        cat = jnp.concatenate(
            [gat_a[a, 2 * p] + gat_a[a, 2 * p + 1] for p in range(GROUP // 2)], axis=1
        )
        got = dot(cat, weight_a[...])
        gat_b[a, q] = halved(got[:, 2 * rank : 4 * rank], q % 2)
        for c in copies_b(gat_b.at[a], b_send.at[a], b_recv.at[a]):
            c.start()
        return got[:, : 2 * rank]

    def cross_round(a, part):
        arrive_b(gat_b.at[a], b_send.at[a], b_recv.at[a])
        cat = jnp.concatenate(
            [gat_b[a, 2 * p] + gat_b[a, 2 * p + 1] for p in range(groups // 2)], axis=1
        )
        total = part + dot(cat, weight_b[...])[:, : 2 * rank]
        return total.astype(BF16)

    def far_loop(a):
        first = me * slots - slots

        def source(i, f):
            return mom[a][jnp.clip(far_idx[f, i] - first, 0, 3 * slots - 1)]

        def step(t, carry):
            got = []
            for u in range(8):
                i = t * 8 + u
                v = jnp.concatenate(
                    [
                        pair(source(i, 2 * p), source(i, 2 * p + 1))
                        for p in range(far_count // 2)
                    ],
                    axis=1,
                )
                got.append(dot(v, far_t[i]).astype(BF16))
            for u in range(8):
                local[t * 8 + u, :, 0:rank] = got[u]
            return carry

        lax.fori_loop(0, slots // 8, step, 0)

    def spread(i, down):
        mask = live_ref[i].astype(F32)
        return (w2[i] + dot(pair(local[i], down), spread_w[i])) * mask

    def fold(x):
        return x[:, : points // 2] + x[:, points // 2 :]

    def pack(parts):
        wide = lax.broadcasted_iota(jnp.int32, (cols, 128), 1)
        total = jnp.zeros((cols, 128), F32)
        for k, p in enumerate(parts):
            total = total + jnp.where(wide == k, jnp.sum(p, axis=1, keepdims=True), 0.0)
        padded = jnp.concatenate([total, jnp.zeros((128 - cols, 128), F32)], axis=0)
        return jnp.transpose(padded)[:8]

    def reduce_first(t, rows):
        red_a[t, j] = rows
        for c in copies_a(red_a.at[t], ra_send.at[t], ra_recv.at[t]):
            c.start()

    def reduce_second(t):
        arrive_a(red_a.at[t], ra_send.at[t], ra_recv.at[t])
        total = red_a[t, 0]
        for k in range(1, GROUP):
            total = total + red_a[t, k]
        red_b[t, q] = total
        for c in copies_b(red_b.at[t], rb_send.at[t], rb_recv.at[t]):
            c.start()

    def reduce_third(t):
        arrive_b(red_b.at[t], rb_send.at[t], rb_recv.at[t])
        total = red_b[t, 0]
        for k in range(1, groups):
            total = total + red_b[t, k]
        return total

    loads[0].wait()

    def start_step(i, acc):
        s = rhs[i] * live_ref[i].astype(F32)
        rhs[i] = s
        v = s.astype(BF16)
        own[0][i] = v
        full[0][reach + i] = v
        return acc + fold(s * s)

    norm_part = lax.fori_loop(0, slots, start_step, jnp.zeros((cols, points // 2), F32))
    pl.semaphore_wait(barrier, GROUP - 1 + groups - 1 + 2)
    halo_start(0, 0)
    loads[1].wait()
    lax.fori_loop(0, slots, transpose_basis, 0)
    moment_loop(0)
    halo_start(0, 1)

    rowi = lax.broadcasted_iota(jnp.int32, (rank, 2 * rank), 0)
    coli = lax.broadcasted_iota(jnp.int32, (rank, 2 * rank), 1)
    eye_twice = jnp.where(rowi == coli % rank, 1.0, 0.0).astype(BF16)
    loads[2].wait()
    twice[...] = dot(transfer[...], eye_twice).astype(BF16)
    box_start(0)
    reduce_first(0, pack([norm_part]))

    loads[3].wait()
    loads[4].wait()

    def node_row(level, node):
        return pl.multiple_of((2 * n - 2 * (n >> level) + node) * rank, rank)

    def node_up(level, node, count):
        return up[pl.ds(node_row(level, node), count * rank), :]

    path = None
    couples = []
    for level in range(levels):
        c = couple[pl.ds(node_row(level, me >> level), rank), :]
        if path is None:
            r4 = lax.broadcasted_iota(jnp.int32, (4 * rank, rank), 0)
            c4 = lax.broadcasted_iota(jnp.int32, (4 * rank, rank), 1)
            path_pad = jnp.where((r4 % rank == c4) & (r4 < 2 * rank), 1.0, 0.0).astype(BF16)
        else:
            blank_rows = jnp.zeros((2 * rank, rank), BF16)
            path_pad = jnp.concatenate([path, path, blank_rows], axis=0)
        couples.append(dot_nt(c, path_pad))
        if level < levels - 1:
            u = node_up(level, me >> level, 1)
            path = u if path is None else dot(path, u).astype(BF16)

    def own_sibling(level, node):
        sibling = (me >> level) ^ 1
        f0 = jnp.where(sibling == node, 1.0, 0.0).astype(F32)
        f1 = jnp.where(sibling == node + 1, 1.0, 0.0).astype(F32)
        return jnp.concatenate([couples[level] * f0, couples[level] * f1], axis=0)

    wide_r = lax.broadcasted_iota(jnp.int32, (rank, 4 * rank), 0)
    wide_c = lax.broadcasted_iota(jnp.int32, (rank, 4 * rank), 1)
    root = jnp.where((wide_c >= 2 * rank) & (wide_r == wide_c % rank), 1.0, 0.0).astype(BF16)
    nodes = [root]
    for level in reversed(range(low)):
        below = []
        for m, x in enumerate(nodes):
            node = (base >> level) + 2 * m
            both = (dot(node_up(level, node, 2), x) + own_sibling(level, node)).astype(BF16)
            below.extend([both[:rank], both[rank:]])
        nodes = below
    for k, x in enumerate(nodes):
        weight_a[k * rank : (k + 1) * rank, :] = x
    nodes = [None]
    for level in reversed(range(low, levels)):
        below = []
        for m, x in enumerate(nodes):
            both = own_sibling(level, 2 * m)
            if x is not None:
                both = both + dot(node_up(level, 2 * m, 2), x)
            both = both.astype(BF16)
            below.extend([both[:rank], both[rank:]])
        nodes = below
    for k, x in enumerate(nodes):
        weight_b[k * rank : (k + 1) * rank, :] = x

    lax.fori_loop(0, slots // 4, spread_weights, 0)

    def operator_middle(a):
        split = reach + 4 * (a + 1)
        near_inner(a, reach, split)
        part = group_round(a)
        if a == 0:
            reduce_second(0)
        near_inner(a, split, slots - reach)
        halo_arrive(a, 0)
        near_rows(a, [0, 1, slots - 2, slots - 1], a == 0, full, reach)
        if a == 0:
            loads[5].wait()
        halo_arrive(a, 1)
        far_loop(a)
        return cross_round(a, part)

    down = operator_middle(0)
    norm_row = jnp.sqrt(reduce_third(0) + epsilon)
    inv_norm = to_columns(1.0 / norm_row)[:cols, 0:1]
    own_square = red_b[0, 0]
    for k in range(1, groups):
        own_square = own_square + red_b[0, k]

    def image_step(t, carry):
        got = [spread(t * 4 + u, down) * inv_norm for u in range(4)]
        for u in range(4):
            i = t * 4 + u
            v = got[u].astype(BF16)
            w1[i] = got[u]
            own[1][i] = v
            full[1][reach + i] = v
        return carry

    lax.fori_loop(0, slots // 4, image_step, 0)
    halo_start(1, 0)
    moment_loop(1)
    halo_start(1, 1)
    box_start(1)
    down = operator_middle(1)

    def gram_step(t, accs):
        got = [spread(t * 4 + u, down) for u in range(4)]
        for u in range(4):
            i = t * 4 + u
            z = got[u]
            w2[i] = z
            b = rhs[i] * inv_norm
            w = w1[i]
            accs = (
                accs[0] + fold(b * w),
                accs[1] + fold(w * w),
                accs[2] + fold(b * z),
                accs[3] + fold(w * z),
                accs[4] + fold(z * z),
            )
        return accs

    zero = jnp.zeros((cols, points // 2), F32)
    accs = lax.fori_loop(0, slots // 4, gram_step, (zero,) * 5)
    reduce_first(1, pack(accs))
    reduce_second(1)
    sums = reduce_third(1)

    norm = norm_row[0:1]
    unit = own_square[0:1] / (norm * norm)
    h, e, f, g, k2 = (sums[k : k + 1] for k in range(5))
    first_square = jnp.maximum(e - 2.0 * h * h + h * h * unit, 0.0)
    length = jnp.sqrt(first_square + epsilon)
    inv_l = 1.0 / length
    cross = (f - h * h) * inv_l
    inner = (g - h * e - h * f + h * h * h) * inv_l * inv_l
    image_square = (k2 - 2.0 * h * g + h * h * e) * inv_l * inv_l
    second_square = (
        image_square
        - 2.0 * cross * cross
        - 2.0 * inner * inner
        + cross * cross * unit
        + inner * inner * first_square * inv_l * inv_l
        + 2.0 * cross * inner * (h - h * unit) * inv_l
    )
    second = jnp.sqrt(jnp.maximum(second_square, 0.0) + epsilon)
    inv_s = 1.0 / second
    alpha = inv_l * inv_s
    beta = -(h + inner) * alpha
    gamma = (inner * h * inv_l - cross) * inv_s / norm
    blank = jnp.zeros((1, 128), F32)
    hess = jnp.concatenate([norm, h, length, cross, inner, second, blank, blank], axis=0)
    hess_ref[...] = hess[:6, :cols]
    coef = to_columns(jnp.concatenate([alpha, beta, gamma] + [blank] * 5, axis=0))
    ca, cb, cg = (coef[:cols, k : k + 1] for k in range(3))

    def out_step(i, carry):
        out_ref[i] = ca * w2[i] + cb * w1[i] + cg * rhs[i]
        return carry

    lax.fori_loop(0, slots, out_step, 0)

    for a in range(2):
        for c in copies_a(gat_a.at[a], a_send.at[a], a_recv.at[a]):
            c.wait_send()
        for c in copies_b(gat_b.at[a], b_send.at[a], b_recv.at[a]):
            c.wait_send()
        for c in copies_a(red_a.at[a], ra_send.at[a], ra_recv.at[a]):
            c.wait_send()
        for c in copies_b(red_b.at[a], rb_send.at[a], rb_recv.at[a]):
            c.wait_send()
        halo_finish(a, 0)
        halo_finish(a, 1)


def on_device(
    right_hand,
    leaf_live,
    near_index,
    near_tile,
    far_index,
    far_couple,
    leaf_basis,
    leaf_transfer,
    tree_up,
    tree_couple,
):
    n = lax.axis_size("leaf")
    slots, cols, points = right_hand.shape
    rank = leaf_basis.shape[1]
    far_count = far_index.shape[1]
    nodes = tree_up.shape[0]
    reach = 2
    groups = n // GROUP
    far_flat = far_couple.reshape(slots, far_count * rank, rank)
    transfer_flat = leaf_transfer.reshape(slots * rank, rank)
    up_flat = tree_up.reshape(nodes * rank, rank)
    couple_flat = tree_couple.reshape(nodes * rank, rank)
    smem = pl.BlockSpec(memory_space=pltpu.SMEM)
    anywhere = pl.BlockSpec(memory_space=pltpu.HBM)
    vmem = pl.BlockSpec(memory_space=pltpu.VMEM)
    dma = pltpu.SemaphoreType.DMA
    return pl.pallas_call(
        functools.partial(kernel, n),
        out_shape=(
            jax.ShapeDtypeStruct((slots, cols, points), F32),
            jax.ShapeDtypeStruct((6, cols), F32),
        ),
        in_specs=[smem] * 3 + [anywhere] * 7,
        out_specs=(vmem, vmem),
        scratch_shapes=[
            pltpu.VMEM((slots, cols, points), F32),
            pltpu.VMEM(near_tile.shape, BF16),
            pltpu.VMEM(far_flat.shape, BF16),
            pltpu.VMEM(leaf_basis.shape, BF16),
            pltpu.VMEM(transfer_flat.shape, BF16),
            pltpu.VMEM(up_flat.shape, BF16),
            pltpu.VMEM(couple_flat.shape, BF16),
            pltpu.VMEM((slots, cols, points), BF16),
            pltpu.VMEM((slots, cols, points), BF16),
            pltpu.VMEM((slots + 2 * reach, cols, points), BF16),
            pltpu.VMEM((slots + 2 * reach, cols, points), BF16),
            pltpu.VMEM((3 * slots, cols, 2 * rank), BF16),
            pltpu.VMEM((3 * slots, cols, 2 * rank), BF16),
            pltpu.VMEM((slots, cols, 2 * rank), BF16),
            pltpu.VMEM((slots, cols, points), F32),
            pltpu.VMEM((slots, cols, points), F32),
            pltpu.VMEM((GROUP * rank, 4 * rank), BF16),
            pltpu.VMEM((groups * rank, 4 * rank), BF16),
            pltpu.VMEM((slots * rank, 2 * rank), BF16),
            pltpu.VMEM((slots, points, 2 * rank), BF16),
            pltpu.VMEM((slots, 2 * rank, points), BF16),
            pltpu.VMEM((2, GROUP, cols, 2 * rank), BF16),
            pltpu.VMEM((2, groups, cols, 2 * rank), BF16),
            pltpu.VMEM((2, GROUP, 8, 128), F32),
            pltpu.VMEM((2, groups, 8, 128), F32),
            dma((6,)),
            dma((slots,)),
            dma((2, 2, 2)),
            dma((2, 2, 2)),
            dma((2, GROUP - 1)),
            dma((2, GROUP - 1)),
            dma((2, groups - 1)),
            dma((2, groups - 1)),
            dma((2, GROUP - 1)),
            dma((2, GROUP - 1)),
            dma((2, groups - 1)),
            dma((2, groups - 1)),
        ],
        compiler_params=pltpu.CompilerParams(
            collective_id=0, has_side_effects=True, vmem_limit_bytes=54400 * 1024
        ),
    )(
        leaf_live,
        near_index.T,
        far_index.T,
        right_hand,
        near_tile,
        far_flat,
        leaf_basis,
        transfer_flat,
        up_flat,
        couple_flat,
    )


def solution(mesh):
    placed = (
        P("leaf", None, None),
        P("leaf"),
        P("leaf", None),
        P("leaf", None, None, None),
        P("leaf", None),
        P("leaf", None, None, None),
        P("leaf", None, None),
        P("leaf", None, None),
        P(),
        P(),
    )
    return jax.shard_map(
        on_device,
        mesh=mesh,
        in_specs=placed,
        out_specs=(P("leaf", None, None), P()),
        check_vma=False,
    )
```
